32 devices in a mesh: groups: 2 (over y), cell: 4 (over z), rep: 2 (over x), sub: 2 (over core).
Axes of the slice: x: 2, y: 2, z: 4, core: 2. Of those that a mesh axis runs over, the one named last changes fastest.
Arguments:
- points: float32 [4, 65536], P(None, ('groups', 'cell', 'rep', 'sub')), parts along dimension 1, may hold values from -4 to 4
- cotangent: float32 [4, 65536], P(None, ('groups', 'cell', 'rep', 'sub')), parts along dimension 1, may hold values from -6 to 6
- cell_ids: int32 [65536, 1], P(('groups', 'cell', 'rep', 'sub')), parts along dimension 0, may hold values from 0 to 31; in each aligned block of 2048 rows (0 to 2047, 2048 to 4095, ...) at most 128 rows name the same one
- camera_ids: int32 [65536], P(('groups', 'cell', 'rep', 'sub')), parts along dimension 0, may hold values from 0 to 63
- valid: int32 [65536], P(('groups', 'cell', 'rep', 'sub')), parts along dimension 0, may hold values 0 or 1
- w_enc: bfloat16 [32, 128, 256], P('cell'), may hold values from -0.5 to 0.5
- w_hidden: bfloat16 [32, 256, 128], P('cell'), may hold values from -0.375 to 0.375
- w_code: bfloat16 [32, 48, 128], P('cell'), may hold values from -0.875 to 0.875
- w_out: bfloat16 [32, 4, 128], P('cell'), may hold values from -0.5 to 0.5
- poses: float32 [3, 256], P(None, 'cell'), may hold values from -3 to 3
- codes: bfloat16 [48, 256], replicated, may hold values from -5 to 5
Outputs:
- grad_w_enc: float32 [64, 128, 256], P(('groups', 'cell')), parts along dimension 0
- grad_w_hidden: float32 [64, 256, 128], P(('groups', 'cell')), parts along dimension 0
- grad_w_code: float32 [64, 48, 128], P(('groups', 'cell')), parts along dimension 0
- grad_w_out: float32 [64, 4, 128], P(('groups', 'cell')), parts along dimension 0
- grad_poses: float32 [3, 512], P(None, ('groups', 'cell')), parts along dimension 1
- grad_codes: float32 [48, 512], P(None, ('groups', 'cell')), parts along dimension 1
The draws below stay inside these ranges and needn't reach their ends.
There are 2 independent parts, one for each index of `groups`. The reference program is written for one: setup_inputs(seed, part) draws one part's arguments, and reference() takes and returns one part's arrays. A program takes and returns all parts, laid end to end along the dimension named above; an argument that names none is the same for every part. Nothing has to cross between parts.
Inputs may be any that keep to these rules, and one draw needn't show every extreme that they name: `cell_ids`: in each device's aligned block of 2048 samples no cell is named more than 128 times, a bound that some block reaches.
All inputs are finite; a program needn't handle non-finite values. No bound on the sum of `valid` on one device may be relied on, other than what follows from the above.
Results may differ from the reference program's by a relative error of at most 0.017.
Values may be sent and summed in bfloat16 or wider, within the bound.
No kernel may reach another device: no remote copies, remote signals or barrier semaphores. Data moves between devices by JAX's collectives and lax.ppermute only.
A program may use at most 64 MiB of HBM per device.

```python
import math
import jax
import jax.numpy as jnp
import numpy as np
from jax import lax

HIDDEN_SIZE = 256
COLOR = 128
CODE = 48
FREQ = 16
ENC = 128
OUT = 4
CELLS = 32
SAMP_DEV = 2048
CAM_DEV = 64
CAMERAS = 256
CAP = 128
SAMPLES = 32768
N_CELL = 4
N_REP = 2
N_SUB = 2


def place_ends(result, rng, least, high):
    longest = result.shape.index(max(result.shape))
    spots = []
    for shift in (0, 1):
        where = [jax.random.randint(jax.random.fold_in(rng, axis), (), 0, length) for axis, length in enumerate(result.shape)]
        where[longest] = (where[longest] + shift) % result.shape[longest]
        spots.append(tuple(where))
    return result.at[spots[0]].set(least).at[spots[1]].set(high)


def levels(rng, extent, pieces, least, largest):
    loudness = 1.0
    for axis_at, blocks in pieces:
        draws = jax.random.uniform(jax.random.fold_in(jax.random.fold_in(rng, 6), axis_at), (blocks,), jnp.float32, least / len(pieces), largest / len(pieces))
        loudness = loudness * jnp.repeat(jnp.exp(draws), extent[axis_at] // blocks).reshape((-1,) + (1,) * (len(extent) - 1 - axis_at))
    return loudness


def deal_out(own_key, own, number, rows, count, top, reach, slope):
    sequence = jax.random.permutation(own_key, count)
    crowded, ordinary = shares(count, rows * top, reach, slope, True), shares(count, rows * top, reach, slope, False)
    places = jnp.arange(count)

    def named(tallies, turn):
        used = int((tallies > 0).sum())
        fixed = max(1, used // 4)
        passed = fixed + (places - fixed + turn * (used - fixed)) % max(1, count - fixed)
        return jnp.zeros((count,), jnp.int32).at[sequence[jnp.where(places < fixed, places, passed)]].set(jnp.asarray(tallies, jnp.int32))

    tallies = jnp.where(number % 4 == 0, named(crowded, number // 4), named(ordinary, number - number // 4 - 1))
    mixed = jax.random.permutation(jax.random.fold_in(own, 3), count)
    donor, sink = mixed[0:count // 2 * 2:2], mixed[1:count // 2 * 2:2]
    room = jnp.minimum(tallies[donor] - 1, reach - tallies[sink]) // 2
    room = jnp.where((donor == sequence[0]) | (sink == sequence[0]) | (tallies[sink] == 0), 0, jnp.maximum(room, 0))
    passed = jax.random.randint(jax.random.fold_in(own, 4), (count // 2,), 0, 1 << 20) % (room + 1)
    tallies = tallies.at[donor].add(-passed).at[sink].add(passed)
    members = jnp.searchsorted(jnp.cumsum(tallies), jnp.arange(rows * top), side="right").astype(jnp.int32)
    table = members.reshape(top, rows).T
    table = table[jax.random.permutation(jax.random.fold_in(own, 1), rows)]
    turn = jax.random.randint(jax.random.fold_in(own, 2), (rows, 1), 0, top)
    return jnp.take_along_axis(table, (jnp.arange(top)[None, :] + turn) % top, axis=1)


def shares(count, total, most, slope, full):
    portions = [(1 << 20) // math.isqrt(grade ** slope) + 1 for grade in range(1, count + 1)]
    largest = most if full else min(most, max(-(-total // count), total * portions[0] // sum(portions)))
    least = 1 if total - largest >= count - 1 else 0
    holding, spare = [largest] + [least] * (count - 1), total - largest - least * (count - 1)
    while spare > 0:
        free = [i for i in range(1, count) if holding[i] < largest] or [i for i in range(1, count) if holding[i] < most]
        whole, left = sum([portions[i] for i in free]), spare
        for i in free:
            addition = min(most - holding[i], max(1, left * portions[i] // whole), spare)
            holding[i] = holding[i] + addition
            spare = spare - addition
    return np.array(holding)


def bell_draw(stream_key, dims, deviation, bound, pieces=(), kind=jnp.bfloat16):
    factor_of = levels(stream_key, dims, pieces, -0.22, 0.18) if pieces else 1.0
    drawn = jax.random.normal(stream_key, dims, jnp.float32) * deviation * factor_of
    return jnp.minimum(jnp.maximum(drawn, -bound), bound).astype(kind)


def setup_inputs(seed: int = 0, part: int = 0) -> dict:
    key_of = jax.random.split(jax.random.key(seed), 12)
    part_keys = jax.random.split(jax.random.fold_in(key_of[11], part), 12)
    points = bell_draw(part_keys[0], (4, SAMPLES), 1.0, 4.0, ((1, 16),), jnp.float32)
    cotangent = bell_draw(part_keys[1], (OUT, SAMPLES), 1.0, 6.0, ((1, 16),), jnp.float32)
    cell_ids_keys = jax.random.split(jax.random.fold_in(part_keys[2], 1), SAMPLES // SAMP_DEV)
    cell_ids_turns = jax.random.permutation(jax.random.fold_in(part_keys[2], 3), SAMPLES // SAMP_DEV)
    cell_ids = jax.vmap(lambda own, number: deal_out(jax.random.fold_in(part_keys[2], 2), own, number, SAMP_DEV, CELLS, 1, CAP, 2))(cell_ids_keys, cell_ids_turns).reshape((SAMPLES, 1))
    camera_ids = place_ends(jax.random.randint(part_keys[3], (SAMPLES,), 0, CAM_DEV), jax.random.fold_in(part_keys[3], 1), 0, CAM_DEV - 1).astype(jnp.int32)
    valid = place_ends((jax.random.randint(part_keys[4], (SAMPLES,), 0, 4) < 3).astype(jnp.int32), jax.random.fold_in(part_keys[4], 1), 0, 1)
    w_enc = bell_draw(key_of[5], (CELLS, ENC, HIDDEN_SIZE), ENC ** -0.5, 0.5, ((0, 4),))
    w_hidden = bell_draw(key_of[6], (CELLS, HIDDEN_SIZE, COLOR), HIDDEN_SIZE ** -0.5, 0.375, ((0, 4),))
    w_code = bell_draw(key_of[7], (CELLS, CODE, COLOR), CODE ** -0.5, 0.875, ((0, 4),))
    w_out = bell_draw(key_of[8], (CELLS, OUT, COLOR), COLOR ** -0.5, 0.5, ((0, 4),))
    poses = bell_draw(key_of[9], (3, CAMERAS), 0.5, 3.0, ((1, 4),), jnp.float32)
    codes = bell_draw(key_of[10], (CODE, CAMERAS), 1.0, 5.0)
    return dict(points=points, cotangent=cotangent, cell_ids=cell_ids, camera_ids=camera_ids, valid=valid, w_enc=w_enc, w_hidden=w_hidden, w_code=w_code, w_out=w_out, poses=poses, codes=codes)


def frequencies():
    return 2.0 ** (jnp.arange(FREQ, dtype=jnp.float32) * 0.25)


def encode(coords):
    angles = coords[:, None, :] * frequencies()[None, :, None]
    stacked = jnp.concatenate([jnp.sin(angles), jnp.cos(angles)], axis=0)
    return stacked.reshape(8 * FREQ, coords.shape[-1])


def chain_coords(grad_encoded, coords):
    angles = coords[:, None, :] * frequencies()[None, :, None]
    halves = grad_encoded.reshape(2, 4, FREQ, coords.shape[-1])
    scaled = frequencies()[None, :, None]
    return jnp.sum(scaled * (halves[0] * jnp.cos(angles) - halves[1] * jnp.sin(angles)), axis=1)


def product(form, left, right):
    return jnp.einsum(form, left.astype(jnp.float32), right.astype(jnp.float32), precision=lax.Precision.HIGHEST)


def cell_backward(encoded, code_rows, tangent, weight_enc, weight_hidden, weight_code, weight_out):
    pre_trunk = product("eh,es->hs", weight_enc, encoded)
    trunk = jax.nn.softplus(pre_trunk).astype(jnp.bfloat16)
    pre_color = product("hc,hs->cs", weight_hidden, trunk) + product("dc,ds->cs", weight_code, code_rows)
    color_act = jax.nn.softplus(pre_color).astype(jnp.bfloat16)
    grad_w_out = product("os,cs->oc", tangent, color_act)
    grad_color = (product("oc,os->cs", weight_out, tangent) * jax.nn.sigmoid(pre_color)).astype(jnp.bfloat16)
    grad_w_hidden = product("hs,cs->hc", trunk, grad_color)
    grad_w_code = product("ds,cs->dc", code_rows, grad_color)
    grad_code_row = product("dc,cs->ds", weight_code, grad_color)
    grad_trunk = (product("hc,cs->hs", weight_hidden, grad_color) * jax.nn.sigmoid(pre_trunk)).astype(jnp.bfloat16)
    grad_w_enc = product("es,hs->eh", encoded, grad_trunk)
    grad_encoded = product("eh,hs->es", weight_enc, grad_trunk)
    return grad_encoded, grad_code_row, grad_w_enc, grad_w_hidden, grad_w_code, grad_w_out


def rank_of(identity):
    one_hot = (identity[:, None] == jnp.arange(CELLS, dtype=jnp.int32)[None, :]).astype(jnp.int32)
    before = jnp.cumsum(one_hot, axis=0) - one_hot
    return jnp.sum(before * one_hot, axis=1).astype(jnp.int32)


def reference(points, cotangent, cell_ids, camera_ids, valid, w_enc, w_hidden, w_code, w_out, poses, codes):
    devices = N_CELL * N_REP * N_SUB
    total_samples = cell_ids.shape[0]
    device_of = (jnp.arange(total_samples, dtype=jnp.int32) // SAMP_DEV).astype(jnp.int32)
    owner_index = device_of // (N_REP * N_SUB)
    camera = (owner_index * CAM_DEV + camera_ids).astype(jnp.int32)
    coords = jnp.concatenate([points[0:3] + poses[:, camera], points[3:4]], axis=0)
    tangent = cotangent * valid.astype(jnp.float32)[None, :]
    cell_of = cell_ids[:, 0].astype(jnp.int32)
    slot_rank = lax.map(rank_of, cell_of.reshape(devices, SAMP_DEV)).reshape(-1)
    width = devices * CAP
    slot_index = (cell_of * width + device_of * CAP + slot_rank).astype(jnp.int32)
    slot_total = CELLS * width
    coord_buffer = jnp.zeros((4, slot_total), jnp.float32).at[:, slot_index].set(coords)
    tangent_buffer = jnp.zeros((OUT, slot_total), jnp.float32).at[:, slot_index].set(tangent)
    image_buffer = jnp.zeros((slot_total,), jnp.int32).at[slot_index].set(camera)
    coord_cells = coord_buffer.reshape(4, CELLS, width).transpose(1, 0, 2)
    tangent_cells = tangent_buffer.reshape(OUT, CELLS, width).transpose(1, 0, 2)
    image_cells = image_buffer.reshape(CELLS, width)

    def per_cell(inputs):
        cell_coords, cell_tangent, cell_images, weight_enc, weight_hidden, weight_code, weight_out = inputs
        encoded = encode(cell_coords).astype(jnp.bfloat16)
        code_rows = codes[:, cell_images]
        grads = cell_backward(encoded, code_rows, cell_tangent, weight_enc, weight_hidden, weight_code, weight_out)
        return (chain_coords(grads[0], cell_coords), grads[1], grads[2], grads[3], grads[4], grads[5])

    grad_coords, grad_code_row, grad_w_enc, grad_w_hidden, grad_w_code, grad_w_out = lax.map(
        per_cell, (coord_cells, tangent_cells, image_cells, w_enc, w_hidden, w_code, w_out))
    coords_back = grad_coords.transpose(1, 0, 2).reshape(4, slot_total)[:, slot_index]
    codes_back = grad_code_row.transpose(1, 0, 2).reshape(CODE, slot_total)[:, slot_index]
    grad_poses = jax.ops.segment_sum(coords_back[0:3].T, camera, num_segments=CAMERAS).T
    grad_codes = jax.ops.segment_sum(codes_back.T, camera, num_segments=CAMERAS).T
    return (grad_w_enc, grad_w_hidden, grad_w_code, grad_w_out, grad_poses, grad_codes)
```

```python
import functools

import jax
import jax.numpy as jnp
from jax import lax
from jax.experimental import pallas as pl
from jax.experimental.pallas import tpu as pltpu
from jax.sharding import PartitionSpec as P

BF16 = jnp.bfloat16
F32 = jnp.float32
VMEM_BYTES = 50 * 1024 * 1024
RECORD = 16
TANGENT_ROW = 8
CAMERA_ROW = 12


def dot_nn(a, b):
    return lax.dot_general(a, b, (((1,), (0,)), ((), ())), preferred_element_type=F32)


def dot_nt(a, b):
    return lax.dot_general(a, b, (((1,), (1,)), ((), ())), preferred_element_type=F32)


def dot_tn(a, b):
    return lax.dot_general(a, b, (((0,), (0,)), ((), ())), preferred_element_type=F32)


def iota(shape, dim):
    return lax.broadcasted_iota(jnp.int32, shape, dim)


def place_kernel(cells_all, cap, n_cell, n_part, me_ref, points_ref, cot_ref, cell_ref, cam_ref,
                 valid_ref, poses_ref, *refs):
    outs, spread = refs[:n_part], refs[n_part]
    n = points_ref.shape[1]
    cams = poses_ref.shape[1]
    lc = cells_all // (n_cell * n_part)
    cam = cam_ref[...]
    cam_hot = (iota((cams, n), 0) == cam).astype(F32).astype(BF16)
    poses = poses_ref[...]
    high = poses.astype(BF16)
    rest = poses - high.astype(F32)
    middle = rest.astype(BF16)
    low = (rest - middle.astype(F32)).astype(BF16)
    offsets = (dot_nn(high, cam_hot) + dot_nn(middle, cam_hot)) + dot_nn(low, cam_hot)
    points = points_ref[...]
    coords = jnp.concatenate([points[0:3] + offsets, points[3:4]], axis=0)
    coords_high = coords.astype(BF16).astype(F32)
    tangent = cot_ref[...] * valid_ref[...].astype(F32)
    record = jnp.concatenate(
        [coords_high, coords - coords_high, tangent, cam.astype(F32), jnp.zeros((3, n), F32)], axis=0
    )
    width = 256
    upper = (iota((width, width), 0) <= iota((width, width), 1)).astype(F32).astype(BF16)
    cell_of = cell_ref[...]
    carry = jnp.zeros((cells_all, 1), F32)
    ranks = []
    for b in range(n // width):
        here = cell_of[:, b * width:(b + 1) * width]
        hot = (iota((cells_all, width), 0) == here).astype(F32)
        counted = dot_nn(hot.astype(BF16), upper) + carry
        ranks.append(jnp.sum(counted * hot, axis=0, keepdims=True) - 1.0)
        carry = counted[:, width - 1:width]
    rank = jnp.concatenate(ranks, axis=1).astype(jnp.int32)
    rank_hot = (iota((cap, n), 0) == rank).astype(F32).astype(BF16)
    for c in range(cells_all):
        spread[c * RECORD:(c + 1) * RECORD, :] = jnp.where(cell_of == c, record, 0.0).astype(BF16)
    me_cell, me_part = me_ref[0], me_ref[1]
    rows = lc * RECORD
    for kp in range(n_part):
        for kc in range(n_cell):
            owner = (me_cell ^ kc) * n_part + (me_part ^ kp)
            start = pl.multiple_of(owner * rows, rows)
            outs[kp][kc] = dot_nt(spread[pl.ds(start, rows), :], rank_hot).astype(BF16)


def sin_cos(x):
    n = jnp.floor(x * 0.6366197723675814 + 0.5)
    r = ((x - n * 1.5703125) - n * 4.837512969970703125e-4) - n * 7.54978995489188216e-8
    z = r * r
    s = r + (r * z) * (-1.6666654611e-1 + z * (8.3321608736e-3 + z * -1.9515295891e-4))
    c = (1.0 - 0.5 * z) + (z * z) * (
        4.166664568298827e-2 + z * (-1.388731625493765e-3 + z * 2.443315711809948e-5))
    q = n.astype(jnp.int32)
    swap = (q & 1) == 1
    sine = jnp.where(swap, c, s)
    cosine = jnp.where(swap, s, c)
    sine = jnp.where((q & 2) == 2, -sine, sine)
    cosine = jnp.where(((q + 1) & 2) == 2, -cosine, cosine)
    return sine, cosine


def double_angle(s, c):
    return 2.0 * s * c, 1.0 - 2.0 * s * s


def soft(x):
    e = jnp.exp(-jnp.abs(x))
    u = 1.0 + e
    plus = jnp.maximum(x, 0.0) + jnp.where(e < 1e-4, e, jnp.log(u))
    r = pl.reciprocal(u, approx=True)
    return plus, jnp.where(x >= 0.0, r, e * r)


def cell_kernel(n_cell, freq_count, has_table, me_ref, codes_ref, w_enc_ref, w_hidden_ref, w_code_ref,
                w_out_ref, *refs):
    arrived = refs[:n_cell]
    at = n_cell
    if has_table:
        table_in = refs[at]
        at += 1
    packed_ref, table_ref = refs[at], refs[at + 1]
    enc_s, gt_s, trunk_s, gc_s, act_s, rec_s = refs[at + 2:]
    width = arrived[0].shape[2]
    cams = codes_ref.shape[2]
    code = codes_ref.shape[1]
    color = w_code_ref.shape[2]
    hidden = w_hidden_ref.shape[1]
    w_enc, w_hidden, w_code, w_out = w_enc_ref[0], w_hidden_ref[0], w_code_ref[0], w_out_ref[0]
    half = freq_count // 2
    scale = jnp.exp2(iota((half, 1), 0).astype(F32) * 0.25)
    top = 2.0 ** (half // 4)
    for kc in range(n_cell):
        cols = slice(kc * width, (kc + 1) * width)
        rec = arrived[kc][0]
        rec_s[:, cols] = rec
        recf = rec.astype(F32)
        coords = recf[0:4] + recf[4:8]
        cam = recf[CAMERA_ROW:CAMERA_ROW + 1].astype(jnp.int32)
        cam_hot = (iota((cams, width), 0) == cam).astype(F32).astype(BF16)
        code_rows = dot_nn(codes_ref[kc], cam_hot).astype(BF16)
        angles = jnp.concatenate([coords[j:j + 1] * scale for j in range(4)], axis=0)
        s1, c1 = sin_cos(angles)
        s2, c2 = s1, c1
        for _ in range(half // 4):
            s2, c2 = double_angle(s2, c2)
        pieces = []
        for a, b in ((s1, s2), (c1, c2)):
            for j in range(4):
                pieces += [a[j * half:(j + 1) * half], b[j * half:(j + 1) * half]]
        encoded = jnp.concatenate(pieces, axis=0).astype(BF16)
        enc_s[:, cols] = encoded
        trunk, slope_trunk = soft(dot_tn(w_enc, encoded))
        trunk = trunk.astype(BF16)
        trunk_s[0:hidden, cols] = trunk
        trunk_s[hidden:, cols] = code_rows
        act, slope_color = soft(dot_tn(w_hidden, trunk) + dot_tn(w_code, code_rows))
        act_s[:, cols] = act.astype(BF16)
        gc = (dot_tn(w_out, rec) * slope_color).astype(BF16)
        gc_s[:, cols] = gc
        gt = (dot_nn(w_hidden, gc) * slope_trunk).astype(BF16)
        gt_s[:, cols] = gt
        grad_code = dot_nn(w_code, gc)
        grad_enc = dot_nn(w_enc, gt)
        sums = []
        for j in range(3):
            a, b = j * 2 * half, (4 + j) * 2 * half
            js = slice(j * half, (j + 1) * half)
            first = grad_enc[a:a + half] * c1[js] - grad_enc[b:b + half] * s1[js]
            second = (grad_enc[a + half:a + 2 * half] * c2[js]
                      - grad_enc[b + half:b + 2 * half] * s2[js])
            sums.append(jnp.sum((first + top * second) * scale, axis=0, keepdims=True))
        row = iota((RECORD, width), 0)
        tail = jnp.where(row == 0, sums[0], jnp.where(row == 1, sums[1], jnp.where(row == 2, sums[2], 0.0)))
        per_sample = jnp.concatenate([grad_code, tail], axis=0).astype(BF16)
        table = dot_nt(per_sample, cam_hot)
        if has_table:
            table = table + table_in[kc]
        table_ref[kc] = table.astype(table_ref.dtype)
    g_enc = dot_nt(enc_s[...], gt_s[...]).astype(BF16)
    enc_rows = g_enc.shape[0]
    at_row = 0
    for part in range(hidden // color):
        packed_ref[at_row:at_row + enc_rows, :] = g_enc[:, part * color:(part + 1) * color]
        at_row += enc_rows
    packed_ref[at_row:at_row + hidden + code, :] = dot_nt(trunk_s[...], gc_s[...]).astype(BF16)
    at_row += hidden + code
    packed_ref[at_row:at_row + RECORD, :] = dot_nt(rec_s[...], act_s[...]).astype(BF16)


def unpack_kernel(lc, n_in, at_ref, *refs):
    ins = refs[:n_in]
    enc_ref, hidden_ref, code_ref, out_ref = refs[n_in:]
    enc_rows, enc_cols = enc_ref.shape[1:]
    hidden, color = hidden_ref.shape[1:]
    code = code_ref.shape[1]
    outs = out_ref.shape[1]
    for i in range(n_in):
        cell = at_ref[i // lc] + i % lc
        src = ins[i]
        row = 0
        for part in range(enc_cols // color):
            enc_ref[cell, :, part * color:(part + 1) * color] = src[row:row + enc_rows, :].astype(F32)
            row += enc_rows
        hidden_ref[cell] = src[row:row + hidden, :].astype(F32)
        row += hidden
        code_ref[cell] = src[row:row + code, :].astype(F32)
        row += code
        out_ref[cell] = src[row:row + RECORD, :].astype(F32)[TANGENT_ROW:TANGENT_ROW + outs]


def whole_spec(shape):
    return pl.BlockSpec(shape, functools.partial(lambda d, *_: (0,) * d, len(shape)))


def exchange(value, axes, count, k):
    if k == 0:
        return value
    return lax.ppermute(value, axes, [(i, i ^ k) for i in range(count)])


def shards(points, cotangent, cell_ids, camera_ids, valid, w_enc, w_hidden, w_code, w_out, poses, codes):
    n_cell, n_rep, n_sub = lax.axis_size("cell"), lax.axis_size("rep"), lax.axis_size("sub")
    n_part = n_rep * n_sub
    part_axes = ("rep", "sub")
    local = w_enc.shape[0]
    lc = local // n_part
    cells_all = local * n_cell
    n = points.shape[1]
    cap = max(2, 2 * n // cells_all)
    enc, hidden = w_enc.shape[1:]
    color = w_hidden.shape[2]
    freq_count = enc // 8
    cams = poses.shape[1]
    code = codes.shape[0]
    width = n_part * cap
    me_cell = lax.axis_index("cell")
    me_part = lax.axis_index(part_axes)
    me = jnp.stack([me_cell, me_part]).astype(jnp.int32)
    params = pltpu.CompilerParams(vmem_limit_bytes=VMEM_BYTES)

    sent = pl.pallas_call(
        functools.partial(place_kernel, cells_all, cap, n_cell, n_part),
        out_shape=[jax.ShapeDtypeStruct((n_cell, lc * RECORD, cap), BF16)] * n_part,
        in_specs=[pl.BlockSpec(memory_space=pltpu.SMEM)] + [pl.BlockSpec(memory_space=pltpu.VMEM)] * 6,
        out_specs=[pl.BlockSpec(memory_space=pltpu.VMEM)] * n_part,
        scratch_shapes=[pltpu.VMEM((cells_all * RECORD, n), BF16)],
        compiler_params=params,
        name="place",
    )(me, points, cotangent, cell_ids.reshape(1, n), camera_ids.reshape(1, n), valid.reshape(1, n), poses)

    order = me_cell ^ jnp.arange(n_cell, dtype=jnp.int32)
    codes_rel = codes.reshape(code, n_cell, cams).transpose(1, 0, 2)[order]
    w_out_rows = jnp.pad(w_out, ((0, 0), (TANGENT_ROW, RECORD - TANGENT_ROW - w_out.shape[1]), (0, 0)))

    near = [exchange(sent[kp], part_axes, n_part, kp) for kp in range(n_part)]
    arrived = []
    for kc in range(n_cell):
        lanes = jnp.concatenate([near[kp][kc] for kp in range(n_part)], axis=-1)
        arrived.append(exchange(lanes.reshape(lc, RECORD, width), "cell", n_cell, kc))

    packed_rows = enc * (hidden // color) + hidden + code + RECORD
    table_rows = code + RECORD
    slots = n_cell * width
    own = []
    table = None
    for j in range(lc):
        last = j == lc - 1
        pick = functools.partial(lambda step, i, me_ref: (me_ref[1] * lc + step, 0, 0), j)
        take = functools.partial(lambda step, i, me_ref: (step, 0, 0), j)
        in_specs = [
            whole_spec((n_cell, code, cams)),
            pl.BlockSpec((1, enc, hidden), pick),
            pl.BlockSpec((1, hidden, color), pick),
            pl.BlockSpec((1, code, color), pick),
            pl.BlockSpec((1, RECORD, color), pick),
        ] + [pl.BlockSpec((1, RECORD, width), take)] * n_cell
        operands = [codes_rel, w_enc, w_hidden, w_code, w_out_rows] + arrived
        if table is not None:
            in_specs.append(whole_spec((n_cell, table_rows, cams)))
            operands.append(table)
        packed, table = pl.pallas_call(
            functools.partial(cell_kernel, n_cell, freq_count, table is not None),
            grid_spec=pltpu.PrefetchScalarGridSpec(
                num_scalar_prefetch=1,
                grid=(1,),
                in_specs=in_specs,
                out_specs=[whole_spec((packed_rows, color)), whole_spec((n_cell, table_rows, cams))],
                scratch_shapes=[
                    pltpu.VMEM((enc, slots), BF16),
                    pltpu.VMEM((hidden, slots), BF16),
                    pltpu.VMEM((hidden + code, slots), BF16),
                    pltpu.VMEM((color, slots), BF16),
                    pltpu.VMEM((color, slots), BF16),
                    pltpu.VMEM((RECORD, slots), BF16),
                ],
            ),
            out_shape=[
                jax.ShapeDtypeStruct((packed_rows, color), BF16),
                jax.ShapeDtypeStruct((n_cell, table_rows, cams), BF16 if last else F32),
            ],
            compiler_params=params,
            name="cell_net",
        )(me, *operands)
        own.append(packed)

    held = [[None] * lc for _ in range(n_part)]
    for j in range(lc):
        for kr in range(n_rep):
            over_rep = exchange(own[j], "rep", n_rep, kr)
            for ks in range(n_sub):
                held[kr * n_sub + ks][j] = exchange(over_rep, "sub", n_sub, ks)
    starts = ((me_part ^ jnp.arange(n_part, dtype=jnp.int32)) * lc).astype(jnp.int32)
    flat = [held[k][j] for k in range(n_part) for j in range(lc)]
    grads = pl.pallas_call(
        functools.partial(unpack_kernel, lc, len(flat)),
        out_shape=[
            jax.ShapeDtypeStruct((local, enc, hidden), F32),
            jax.ShapeDtypeStruct((local, hidden, color), F32),
            jax.ShapeDtypeStruct((local, code, color), F32),
            jax.ShapeDtypeStruct((local, w_out.shape[1], color), F32),
        ],
        in_specs=[pl.BlockSpec(memory_space=pltpu.SMEM)]
        + [pl.BlockSpec(memory_space=pltpu.VMEM)] * len(flat),
        out_specs=[pl.BlockSpec(memory_space=pltpu.VMEM)] * 4,
        compiler_params=params,
        name="unpack",
    )(starts, *flat)

    mine = sum(exchange(table[kc], "cell", n_cell, kc).astype(F32) for kc in range(n_cell))
    mine = mine.astype(BF16)
    total = sum(exchange(mine, part_axes, n_part, kp).astype(F32) for kp in range(n_part))
    return (*grads, total[code:code + 3], total[0:code])


def solution(mesh):
    samples = ("groups", "cell", "rep", "sub")
    in_specs = (
        P(None, samples),
        P(None, samples),
        P(samples, None),
        P(samples),
        P(samples),
        P("cell", None, None),
        P("cell", None, None),
        P("cell", None, None),
        P("cell", None, None),
        P(None, "cell"),
        P(),
    )
    out_specs = (
        P(("groups", "cell"), None, None),
        P(("groups", "cell"), None, None),
        P(("groups", "cell"), None, None),
        P(("groups", "cell"), None, None),
        P(None, ("groups", "cell")),
        P(None, ("groups", "cell")),
    )
    return jax.shard_map(shards, mesh=mesh, in_specs=in_specs, out_specs=out_specs, check_vma=False)
```

```python
import functools

import jax
import jax.numpy as jnp
from jax import lax
from jax.experimental import pallas as pl
from jax.experimental.pallas import tpu as pltpu
from jax.sharding import PartitionSpec as P

BF16 = jnp.bfloat16
F32 = jnp.float32
VMEM_BYTES = 32 * 1024 * 1024
ALL_VMEM_BYTES = 64 * 1024 * 1024
SLACK_BYTES = 128 * 1024
PART_AXES = ("rep", "sub")
RECORD = 16
TANGENT_ROW = 8
CAMERA_ROW = 12


def dot_nn(a, b):
    return lax.dot_general(a, b, (((1,), (0,)), ((), ())), preferred_element_type=F32)


def dot_nt(a, b):
    return lax.dot_general(a, b, (((1,), (1,)), ((), ())), preferred_element_type=F32)


def dot_tn(a, b):
    return lax.dot_general(a, b, (((0,), (0,)), ((), ())), preferred_element_type=F32)


def iota(shape, dim):
    return lax.broadcasted_iota(jnp.int32, shape, dim)


def me():
    return lax.axis_index("cell"), lax.axis_index(PART_AXES)


def place_kernel(cells_all, cap, n_cell, n_part, *refs):
    sources, weights, outs, own = refs[:6], refs[6:9], refs[9:9 + n_part], refs[9 + n_part:12 + n_part]
    arrays, (spread, placed, sems) = refs[12 + n_part:18 + n_part], refs[18 + n_part:]
    points_ref, cot_ref, cell_ref, cam_ref, valid_ref, poses_ref = arrays
    me_cell, me_part = me()
    lc = cells_all // (n_cell * n_part)
    pairs = list(zip(sources, arrays)) + [
        (source.at[pl.ds(me_part * lc, lc)], target) for source, target in zip(weights, own)
    ]
    copies = [pltpu.make_async_copy(source, target, sems.at[i]) for i, (source, target) in enumerate(pairs)]
    for copy in copies:
        copy.start()
    for copy in copies[:6]:
        copy.wait()
    n = points_ref.shape[1]
    cams = poses_ref.shape[1]
    cam = cam_ref[...]
    cam_hot = (iota((cams, n), 0) == cam).astype(F32).astype(BF16)
    poses = poses_ref[...]
    high = poses.astype(BF16).astype(F32)
    middle = (poses - high).astype(BF16).astype(F32)
    parts = jnp.concatenate([high, middle, poses - high - middle], axis=0).astype(BF16)
    moved = dot_nn(parts, cam_hot)
    offsets = (moved[0:3] + moved[3:6]) + moved[6:9]
    points = points_ref[...]
    coords = jnp.concatenate([points[0:3] + offsets, points[3:4]], axis=0)
    coords_high = coords.astype(BF16).astype(F32)
    tangent = cot_ref[...] * valid_ref[...].astype(F32)
    record = jnp.concatenate(
        [coords_high, coords - coords_high, tangent, cam.astype(F32), jnp.zeros((3, n), F32)], axis=0
    )
    width = min(256, n)
    blocks = n // width
    upper = (iota((width, width), 0) <= iota((width, width), 1)).astype(F32).astype(BF16)
    cell_of = cell_ref[...]
    hots = [
        (iota((cells_all, width), 0) == cell_of[:, b * width:(b + 1) * width]).astype(F32)
        for b in range(blocks)
    ]
    counts = dot_nn(jnp.concatenate(hots, axis=0).astype(BF16), upper)
    carry = jnp.zeros((cells_all, 1), F32)
    ranks = []
    for b in range(blocks):
        counted = counts[b * cells_all:(b + 1) * cells_all]
        ranks.append(jnp.sum((counted + carry) * hots[b], axis=0, keepdims=True) - 1.0)
        carry = carry + counted[:, width - 1:width]
    rank = jnp.concatenate(ranks, axis=1).astype(jnp.int32)
    rank_hot = (iota((cap, n), 0) == rank).astype(F32).astype(BF16)
    cell_rows = jnp.broadcast_to(cell_of, (RECORD, n))
    for c in range(cells_all):
        spread[c * RECORD:(c + 1) * RECORD, :] = jnp.where(cell_rows == c, record, 0.0).astype(BF16)
    placed[...] = dot_nt(spread[...], rank_hot).astype(BF16)
    rows = lc * RECORD
    for kp in range(n_part):
        for kc in range(n_cell):
            owner = (me_cell ^ kc) * n_part + (me_part ^ kp)
            start = pl.multiple_of(owner * rows, rows)
            outs[kp][kc] = placed[pl.ds(start, rows), :]
    for copy in copies[6:]:
        copy.wait()


def sin_cos(x):
    n = jnp.floor(x * 0.6366197723675814 + 0.5)
    r = ((x - n * 1.5703125) - n * 4.837512969970703125e-4) - n * 7.54978995489188216e-8
    z = r * r
    s = r + (r * z) * (-1.6666654611e-1 + z * (8.3321608736e-3 + z * -1.9515295891e-4))
    c = (1.0 - 0.5 * z) + (z * z) * (
        4.166664568298827e-2 + z * (-1.388731625493765e-3 + z * 2.443315711809948e-5))
    q = n.astype(jnp.int32)
    swap = (q & 1) == 1
    sine = jnp.where(swap, c, s)
    cosine = jnp.where(swap, s, c)
    sine = jnp.where((q & 2) == 2, -sine, sine)
    cosine = jnp.where(((q + 1) & 2) == 2, -cosine, cosine)
    return sine, cosine


def double_angle(s, c):
    return 2.0 * s * c, 1.0 - 2.0 * s * s


def soft(x):
    e = jnp.exp(-jnp.abs(x))
    u = 1.0 + e
    plus = jnp.maximum(x, 0.0) + jnp.where(e < 1e-4, e, jnp.log(u))
    r = pl.reciprocal(u, approx=True)
    return plus, jnp.where(x >= 0.0, r, e * r)


def backward_samples(n_cell, freq_count, codes_ref, w_out, weights, arrived, table_in, table_ref, kept, j):
    enc_s, gt_s, trunk_s, gc_s, act_s, rec_s = kept
    w_enc, w_hidden, w_code = weights
    width = arrived[0].shape[2]
    cams = codes_ref.shape[2]
    hidden = w_hidden.shape[0]
    half = freq_count // 2
    scale = jnp.exp2(iota((half, 1), 0).astype(F32) * 0.25)
    top = 2.0 ** (half // 4)
    for kc in range(n_cell):
        cols = slice(kc * width, (kc + 1) * width)
        rec = arrived[kc][j]
        rec_s[:, cols] = rec
        recf = rec.astype(F32)
        coords = recf[0:4] + recf[4:8]
        cam = recf[CAMERA_ROW:CAMERA_ROW + 1].astype(jnp.int32)
        cam_hot = (iota((cams, width), 0) == cam).astype(F32).astype(BF16)
        code_rows = dot_nn(codes_ref[kc], cam_hot).astype(BF16)
        angles = jnp.concatenate([coords[i:i + 1] * scale for i in range(4)], axis=0)
        s1, c1 = sin_cos(angles)
        s2, c2 = s1, c1
        for _ in range(half // 4):
            s2, c2 = double_angle(s2, c2)
        pieces = []
        for a, b in ((s1, s2), (c1, c2)):
            for i in range(4):
                pieces += [a[i * half:(i + 1) * half], b[i * half:(i + 1) * half]]
        encoded = jnp.concatenate(pieces, axis=0).astype(BF16)
        enc_s[:, cols] = encoded
        trunk, slope_trunk = soft(dot_tn(w_enc, encoded))
        trunk = trunk.astype(BF16)
        trunk_s[0:hidden, cols] = trunk
        trunk_s[hidden:, cols] = code_rows
        act, slope_color = soft(dot_tn(w_hidden, trunk) + dot_tn(w_code, code_rows))
        act_s[:, cols] = act.astype(BF16)
        gc = (dot_tn(w_out, rec) * slope_color).astype(BF16)
        gc_s[:, cols] = gc
        gt = (dot_nn(w_hidden, gc) * slope_trunk).astype(BF16)
        gt_s[:, cols] = gt
        grad_code = dot_nn(w_code, gc)
        grad_enc = dot_nn(w_enc, gt)
        sums = []
        for i in range(3):
            a, b = i * 2 * half, (4 + i) * 2 * half
            at = slice(i * half, (i + 1) * half)
            first = grad_enc[a:a + half] * c1[at] - grad_enc[b:b + half] * s1[at]
            second = (grad_enc[a + half:a + 2 * half] * c2[at]
                      - grad_enc[b + half:b + 2 * half] * s2[at])
            sums.append(jnp.sum((first + top * second) * scale, axis=0, keepdims=True))
        row = iota((RECORD, width), 0)
        tail = jnp.where(row == 0, sums[0], jnp.where(row == 1, sums[1], jnp.where(row == 2, sums[2], 0.0)))
        per_sample = jnp.concatenate([grad_code, tail], axis=0).astype(BF16)
        table = dot_nt(per_sample, cam_hot)
        if table_in is not None:
            table = table + table_in[kc]
        table_ref[kc] = table.astype(table_ref.dtype)


def sum_weights(kept, packed_ref):
    enc_s, gt_s, trunk_s, gc_s, act_s, rec_s = kept
    color = gc_s.shape[0]
    g_enc = dot_nt(enc_s[...], gt_s[...]).astype(BF16)
    enc_rows = g_enc.shape[0]
    row = 0
    for part in range(g_enc.shape[1] // color):
        packed_ref[row:row + enc_rows, :] = g_enc[:, part * color:(part + 1) * color]
        row += enc_rows
    rows = trunk_s.shape[0]
    packed_ref[row:row + rows, :] = dot_nt(trunk_s[...], gc_s[...]).astype(BF16)
    row += rows
    packed_ref[row:row + RECORD, :] = dot_nt(rec_s[...], act_s[...]).astype(BF16)


def cells_kernel(n_cell, freq_count, lc, codes_ref, w_out_ref, *refs):
    weights, arrived, refs = refs[:3], refs[3:3 + n_cell], refs[3 + n_cell:]
    packed_ref, table_ref, kept, sums = refs[0], refs[1], refs[2:8], refs[8]
    rows = packed_ref.shape[0] // lc
    me_part = lax.axis_index(PART_AXES)
    for j in range(lc):
        backward_samples(n_cell, freq_count, codes_ref, w_out_ref[me_part * lc + j], [w[j] for w in weights],
                         arrived, sums if j else None, table_ref if j == lc - 1 else sums,
                         [k.at[j] for k in kept], j)
        sum_weights([k.at[j] for k in kept], packed_ref.at[j * rows:(j + 1) * rows])


def shard_sum_kernel(count, *refs):
    total = refs[0][0].astype(F32)
    for k in range(1, count):
        total = total + refs[k][...].astype(F32)
    refs[count][...] = total.astype(BF16)


def relay_kernel(n_rep, *refs):
    parts, packed_ref, out_ref = refs[:n_rep], refs[n_rep], refs[n_rep + 1]
    total = sum(part[...].astype(F32) for part in parts)
    rows, cams = total.shape
    out_ref[0:packed_ref.shape[0], :] = packed_ref[...]
    total = jnp.concatenate([total, jnp.zeros((rows, out_ref.shape[1] - cams), F32)], axis=1)
    out_ref[packed_ref.shape[0]:, :] = total.astype(BF16)


def unpack_kernel(places, lc, n_prev, packed_rows, tables_at, *refs):
    ins, refs = refs[:len(places)], refs[len(places):]
    if tables_at:
        here, refs = refs[0], refs[1:]
    outs, refs = refs[n_prev:n_prev + 4], refs[n_prev + 4:]
    code = outs[2].shape[1]
    if tables_at:
        cams = refs[0].shape[1]
        first = lc * packed_rows
        total = here[first:, :].astype(F32)
        for i in tables_at:
            total = total + ins[i][first:, :].astype(F32)
        refs[0][...] = total[code:code + 3, 0:cams]
        refs[1][...] = total[0:code, 0:cams]
        refs = refs[2:]
    wide, sems = refs[:-1], refs[-1]
    enc_v, hidden_v, code_v, out_v = wide
    enc_rows, enc_cols = enc_v.shape[1:]
    hidden, color = hidden_v.shape[1:]
    out_rows = out_v.shape[1]
    me_part = lax.axis_index(PART_AXES)
    copies = []
    for i in range(len(places) * lc):
        cell = (me_part ^ places[i // lc]) * lc + i % lc
        src = ins[i // lc]
        row = i % lc * packed_rows
        for part in range(enc_cols // color):
            enc_v[i, :, part * color:(part + 1) * color] = src[row:row + enc_rows, :].astype(F32)
            row += enc_rows
        hidden_v[i] = src[row:row + hidden, :].astype(F32)
        row += hidden
        code_v[i] = src[row:row + code, :].astype(F32)
        row += code
        out_v[i] = src[row:row + RECORD, :].astype(F32)[TANGENT_ROW:TANGENT_ROW + out_rows]
        for m in range(4):
            copy = pltpu.make_async_copy(wide[m].at[i], outs[m].at[cell], sems.at[i, m])
            copy.start()
            copies.append(copy)
    for copy in copies:
        copy.wait()


def cost(us):
    return pl.CostEstimate(flops=us * 10 ** 9, bytes_accessed=us * 3 * 10 ** 6, transcendentals=0)


def exchange(value, axes, count, k):
    if k == 0:
        return value
    return lax.ppermute(value, axes, [(i, i ^ k) for i in range(count)])


def shards(points, cotangent, cell_ids, camera_ids, valid, w_enc, w_hidden, w_code, w_out, poses, codes):
    n_cell, n_rep, n_sub = lax.axis_size("cell"), lax.axis_size("rep"), lax.axis_size("sub")
    n_part = n_rep * n_sub
    local = w_enc.shape[0]
    lc = local // n_part
    cells_all = local * n_cell
    n = points.shape[1]
    cap = max(2, 2 * n // cells_all)
    enc, hidden = w_enc.shape[1:]
    color = w_hidden.shape[2]
    freq_count = enc // 8
    cams = poses.shape[1]
    code = codes.shape[0]
    width = n_part * cap
    params = pltpu.CompilerParams(vmem_limit_bytes=VMEM_BYTES)
    vmem = pl.BlockSpec(memory_space=pltpu.VMEM)
    hbm = pl.BlockSpec(memory_space=pltpu.HBM)

    inputs = (points, cotangent, cell_ids.reshape(1, n), camera_ids.reshape(1, n), valid.reshape(1, n), poses)
    weights = (w_enc, w_hidden, w_code)
    out_shape = [jax.ShapeDtypeStruct((n_cell, lc * RECORD, cap), BF16)] * n_part + [
        jax.ShapeDtypeStruct((lc,) + w.shape[1:], BF16) for w in weights
    ]
    room = sum(2 * a.size // a.shape[-1] * max(a.shape[-1], 128) for a in out_shape) + SLACK_BYTES
    placed = pl.pallas_call(
        functools.partial(place_kernel, cells_all, cap, n_cell, n_part),
        out_shape=out_shape,
        in_specs=[hbm] * 9,
        out_specs=[vmem] * len(out_shape),
        scratch_shapes=[pltpu.VMEM(a.shape, a.dtype) for a in inputs] + [
            pltpu.VMEM((cells_all * RECORD, n), BF16),
            pltpu.VMEM((cells_all * RECORD, cap), BF16),
            pltpu.SemaphoreType.DMA((9,)),
        ],
        compiler_params=pltpu.CompilerParams(vmem_limit_bytes=ALL_VMEM_BYTES - room),
        cost_estimate=cost(3),
        name="place",
    )(*inputs, *weights)
    sent, own_weights = placed[:n_part], placed[n_part:]

    order = lax.axis_index("cell") ^ jnp.arange(n_cell, dtype=jnp.int32)
    codes_rel = codes.reshape(code, n_cell, cams).transpose(1, 0, 2)[order]
    w_out_rows = jnp.pad(w_out, ((0, 0), (TANGENT_ROW, RECORD - TANGENT_ROW - w_out.shape[1]), (0, 0)))

    near = [exchange(sent[kp], PART_AXES, n_part, kp) for kp in range(n_part)]
    arrived = []
    for kc in range(n_cell):
        lanes = jnp.concatenate([near[kp][kc] for kp in range(n_part)], axis=-1)
        arrived.append(exchange(lanes.reshape(lc, RECORD, width), "cell", n_cell, kc))

    packed_rows = enc * (hidden // color) + hidden + code + RECORD
    slots = n_cell * width
    kept_rows = (enc, hidden, hidden + code, color, color, RECORD)
    table_shape = (n_cell, code + RECORD, cams)
    packed, table = pl.pallas_call(
        functools.partial(cells_kernel, n_cell, freq_count, lc),
        in_specs=[vmem] * (5 + n_cell),
        out_specs=[vmem, vmem],
        out_shape=[
            jax.ShapeDtypeStruct((lc * packed_rows, color), BF16),
            jax.ShapeDtypeStruct(table_shape, BF16),
        ],
        scratch_shapes=[pltpu.VMEM((lc, r, slots), BF16) for r in kept_rows] + [pltpu.VMEM(table_shape, F32)],
        compiler_params=params,
        cost_estimate=cost(10),
        name="cells",
    )(codes_rel, w_out_rows, *own_weights, *arrived)

    over_rep = [exchange(packed, "rep", n_rep, kr) for kr in range(n_rep)]
    tables = [table] + [exchange(table[kc], "cell", n_cell, kc) for kc in range(1, n_cell)]
    mine = pl.pallas_call(
        functools.partial(shard_sum_kernel, n_cell),
        in_specs=[vmem] * n_cell,
        out_specs=vmem,
        out_shape=jax.ShapeDtypeStruct(table_shape[1:], BF16),
        compiler_params=params,
        cost_estimate=cost(0),
        name="shard_sum",
    )(*tables)
    parts = [exchange(mine, "rep", n_rep, kr) for kr in range(n_rep)]
    relayed = pl.pallas_call(
        functools.partial(relay_kernel, n_rep),
        in_specs=[vmem] * (n_rep + 1),
        out_specs=vmem,
        out_shape=jax.ShapeDtypeStruct((lc * packed_rows + table_shape[1], color), BF16),
        compiler_params=params,
        cost_estimate=cost(0),
        name="relay",
    )(*parts, over_rep[1])

    early, late = [], []
    for kr in range(n_rep):
        for ks in range(n_sub):
            sent_on = relayed if kr == 1 and ks else over_rep[kr]
            (late if kr and ks else early).append((kr * n_sub + ks, exchange(sent_on, "sub", n_sub, ks)))
    shapes = [
        jax.ShapeDtypeStruct((local, enc, hidden), F32),
        jax.ShapeDtypeStruct((local, hidden, color), F32),
        jax.ShapeDtypeStruct((local, code, color), F32),
        jax.ShapeDtypeStruct((local, w_out.shape[1], color), F32),
    ]
    grads = []
    for group in (early, late):
        tables_at, sums_shape, here = (), [], []
        if group is late:
            tables_at = tuple(i for i, (place, _) in enumerate(group) if place // n_sub == 1)
            sums_shape = [jax.ShapeDtypeStruct((rows, cams), F32) for rows in (3, code)]
            here = [relayed]
        grads = pl.pallas_call(
            functools.partial(
                unpack_kernel, tuple(place for place, _ in group), lc, len(grads), packed_rows, tables_at
            ),
            out_shape=shapes + sums_shape,
            in_specs=[vmem] * (len(group) + len(here)) + [hbm] * len(grads),
            out_specs=[hbm] * 4 + [vmem] * len(sums_shape),
            scratch_shapes=[pltpu.VMEM((len(group) * lc,) + a.shape[1:], F32) for a in shapes]
            + [pltpu.SemaphoreType.DMA((len(group) * lc, 4))],
            input_output_aliases={len(group) + len(here) + i: i for i in range(len(grads))},
            compiler_params=params,
            cost_estimate=cost(0),
            name="unpack",
        )(*[value for _, value in group], *here, *grads)
    return tuple(grads)


def solution(mesh):
    samples = ("groups", "cell", "rep", "sub")
    in_specs = (
        P(None, samples),
        P(None, samples),
        P(samples, None),
        P(samples),
        P(samples),
        P("cell", None, None),
        P("cell", None, None),
        P("cell", None, None),
        P("cell", None, None),
        P(None, "cell"),
        P(),
    )
    out_specs = (
        P(("groups", "cell"), None, None),
        P(("groups", "cell"), None, None),
        P(("groups", "cell"), None, None),
        P(("groups", "cell"), None, None),
        P(None, ("groups", "cell")),
        P(None, ("groups", "cell")),
    )
    return jax.shard_map(shards, mesh=mesh, in_specs=in_specs, out_specs=out_specs, check_vma=False)
```

```python
import functools

import jax
import jax.numpy as jnp
from jax import lax
from jax.experimental import pallas as pl
from jax.experimental.pallas import tpu as pltpu
from jax.sharding import PartitionSpec as P

BF16 = jnp.bfloat16
F32 = jnp.float32
VMEM_BYTES = 32 * 1024 * 1024
ALL_VMEM_BYTES = 64 * 1024 * 1024
SLACK_BYTES = 128 * 1024
PART_AXES = ("rep", "sub")
RECORD = 16
TANGENT_ROW = 8
CAMERA_ROW = 12


def dot_nn(a, b):
    return lax.dot_general(a, b, (((1,), (0,)), ((), ())), preferred_element_type=F32)


def dot_nt(a, b):
    return lax.dot_general(a, b, (((1,), (1,)), ((), ())), preferred_element_type=F32)


def dot_tn(a, b):
    return lax.dot_general(a, b, (((0,), (0,)), ((), ())), preferred_element_type=F32)


def iota(shape, dim):
    return lax.broadcasted_iota(jnp.int32, shape, dim)


def place_kernel(cells_all, cap, n_cell, n_part, *refs):
    sources, weights, placed, own = refs[:6], refs[6:9], refs[9], refs[10:13]
    arrays, (spread, sems) = refs[13:19], refs[19:]
    points_ref, cot_ref, cell_ref, cam_ref, valid_ref, poses_ref = arrays
    me_part = lax.axis_index(PART_AXES)
    lc = cells_all // (n_cell * n_part)
    pairs = list(zip(sources, arrays)) + [
        (source.at[pl.ds(me_part * lc, lc)], target) for source, target in zip(weights, own)
    ]
    copies = [pltpu.make_async_copy(source, target, sems.at[i]) for i, (source, target) in enumerate(pairs)]
    for copy in copies:
        copy.start()
    for copy in copies[:6]:
        copy.wait()
    n = points_ref.shape[1]
    cams = poses_ref.shape[1]
    cam = cam_ref[...]
    cam_hot = (iota((cams, n), 0) == cam).astype(F32).astype(BF16)
    poses = poses_ref[...]
    high = poses.astype(BF16).astype(F32)
    middle = (poses - high).astype(BF16).astype(F32)
    parts = jnp.concatenate([high, middle, poses - high - middle], axis=0).astype(BF16)
    moved = dot_nn(parts, cam_hot)
    offsets = (moved[0:3] + moved[3:6]) + moved[6:9]
    points = points_ref[...]
    coords = jnp.concatenate([points[0:3] + offsets, points[3:4]], axis=0)
    coords_high = coords.astype(BF16).astype(F32)
    tangent = cot_ref[...] * valid_ref[...].astype(F32)
    record = jnp.concatenate(
        [coords_high, coords - coords_high, tangent, cam.astype(F32), jnp.zeros((3, n), F32)], axis=0
    )
    width = min(256, n)
    blocks = n // width
    upper = (iota((width, width), 0) <= iota((width, width), 1)).astype(F32).astype(BF16)
    cell_of = cell_ref[...]
    hots = [
        (iota((cells_all, width), 0) == cell_of[:, b * width:(b + 1) * width]).astype(F32)
        for b in range(blocks)
    ]
    counts = dot_nn(jnp.concatenate(hots, axis=0).astype(BF16), upper)
    carry = jnp.zeros((cells_all, 1), F32)
    ranks = []
    for b in range(blocks):
        counted = counts[b * cells_all:(b + 1) * cells_all]
        ranks.append(jnp.sum((counted + carry) * hots[b], axis=0, keepdims=True) - 1.0)
        carry = carry + counted[:, width - 1:width]
    rank = jnp.concatenate(ranks, axis=1).astype(jnp.int32)
    rank_hot = (iota((cap, n), 0) == rank).astype(F32).astype(BF16)
    cell_rows = jnp.broadcast_to(cell_of, (RECORD, n))
    for c in range(cells_all):
        spread[c * RECORD:(c + 1) * RECORD, :] = jnp.where(cell_rows == c, record, 0.0).astype(BF16)
    placed[...] = dot_nt(spread[...], rank_hot).astype(BF16)
    for copy in copies[6:]:
        copy.wait()


def sin_cos(x):
    n = jnp.floor(x * 0.6366197723675814 + 0.5)
    r = ((x - n * 1.5703125) - n * 4.837512969970703125e-4) - n * 7.54978995489188216e-8
    z = r * r
    s = r + (r * z) * (-1.6666654611e-1 + z * (8.3321608736e-3 + z * -1.9515295891e-4))
    c = (1.0 - 0.5 * z) + (z * z) * (
        4.166664568298827e-2 + z * (-1.388731625493765e-3 + z * 2.443315711809948e-5))
    q = n.astype(jnp.int32)
    swap = (q & 1) == 1
    sine = jnp.where(swap, c, s)
    cosine = jnp.where(swap, s, c)
    sine = jnp.where((q & 2) == 2, -sine, sine)
    cosine = jnp.where(((q + 1) & 2) == 2, -cosine, cosine)
    return sine, cosine


def double_angle(s, c):
    return 2.0 * s * c, 1.0 - 2.0 * s * s


def soft(x):
    e = jnp.exp(-jnp.abs(x))
    u = 1.0 + e
    plus = jnp.maximum(x, 0.0) + jnp.where(e < 1e-4, e, jnp.log(u))
    r = pl.reciprocal(u, approx=True)
    return plus, jnp.where(x >= 0.0, r, e * r)


def fold(table, rows):
    return jnp.concatenate([table[r:r + rows] for r in range(0, table.shape[0], rows)], axis=1)


def backward_samples(n_cell, freq_count, codes_ref, w_out, weights, arrived, table_in, table_ref, kept, j):
    enc_s, gt_s, trunk_s, gc_s, act_s, rec_s = kept
    w_enc, w_hidden, w_code = weights
    blocks = arrived.shape[0] // n_cell
    width = blocks * arrived.shape[2]
    cams = codes_ref.shape[2]
    hidden = w_hidden.shape[0]
    half = freq_count // 2
    scale = jnp.exp2(iota((half, 1), 0).astype(F32) * 0.25)
    top = 2.0 ** (half // 4)
    for kc in range(n_cell):
        cols = slice(kc * width, (kc + 1) * width)
        rec = jnp.concatenate(
            [arrived[kc * blocks + b, j * RECORD:(j + 1) * RECORD, :] for b in range(blocks)], axis=1
        )
        rec_s[:, cols] = rec
        recf = rec.astype(F32)
        coords = recf[0:4] + recf[4:8]
        cam = recf[CAMERA_ROW:CAMERA_ROW + 1].astype(jnp.int32)
        cam_hot = (iota((cams, width), 0) == cam).astype(F32).astype(BF16)
        code_rows = dot_nn(codes_ref[kc], cam_hot).astype(BF16)
        angles = jnp.concatenate([coords[i:i + 1] * scale for i in range(4)], axis=0)
        s1, c1 = sin_cos(angles)
        s2, c2 = s1, c1
        for _ in range(half // 4):
            s2, c2 = double_angle(s2, c2)
        pieces = []
        for a, b in ((s1, s2), (c1, c2)):
            for i in range(4):
                pieces += [a[i * half:(i + 1) * half], b[i * half:(i + 1) * half]]
        encoded = jnp.concatenate(pieces, axis=0).astype(BF16)
        enc_s[:, cols] = encoded
        trunk, slope_trunk = soft(dot_tn(w_enc, encoded))
        trunk = trunk.astype(BF16)
        trunk_s[0:hidden, cols] = trunk
        trunk_s[hidden:, cols] = code_rows
        act, slope_color = soft(dot_tn(w_hidden, trunk) + dot_tn(w_code, code_rows))
        act_s[:, cols] = act.astype(BF16)
        gc = (dot_tn(w_out, rec) * slope_color).astype(BF16)
        gc_s[:, cols] = gc
        gt = (dot_nn(w_hidden, gc) * slope_trunk).astype(BF16)
        gt_s[:, cols] = gt
        grad_code = dot_nn(w_code, gc)
        grad_enc = dot_nn(w_enc, gt)
        sums = []
        for i in range(3):
            a, b = i * 2 * half, (4 + i) * 2 * half
            at = slice(i * half, (i + 1) * half)
            first = grad_enc[a:a + half] * c1[at] - grad_enc[b:b + half] * s1[at]
            second = (grad_enc[a + half:a + 2 * half] * c2[at]
                      - grad_enc[b + half:b + 2 * half] * s2[at])
            sums.append(jnp.sum((first + top * second) * scale, axis=0, keepdims=True))
        row = iota((RECORD, width), 0)
        tail = jnp.where(row == 0, sums[0], jnp.where(row == 1, sums[1], jnp.where(row == 2, sums[2], 0.0)))
        per_sample = jnp.concatenate([grad_code, tail], axis=0).astype(BF16)
        table = dot_nt(per_sample, cam_hot)
        if table_in is not None:
            table = table + table_in[kc]
        copies = table_ref.shape[0] // n_cell
        for i in range(copies):
            table_ref[kc * copies + i] = fold(table, table_ref.shape[1]).astype(table_ref.dtype)


def sum_weights(kept, packed_ref):
    enc_s, gt_s, trunk_s, gc_s, act_s, rec_s = kept
    color = gc_s.shape[0]
    g_enc = dot_nt(enc_s[...], gt_s[...]).astype(BF16)
    enc_rows = g_enc.shape[0]
    row = 0
    for part in range(g_enc.shape[1] // color):
        packed_ref[row:row + enc_rows, :] = g_enc[:, part * color:(part + 1) * color]
        row += enc_rows
    rows = trunk_s.shape[0]
    packed_ref[row:row + rows, :] = dot_nt(trunk_s[...], gc_s[...]).astype(BF16)
    row += rows
    packed_ref[row:row + RECORD, :] = dot_nt(rec_s[...], act_s[...]).astype(BF16)


def cells_kernel(n_cell, freq_count, lc, codes_ref, w_out_ref, *refs):
    weights, arrived = refs[:3], refs[3]
    packed_ref, table_ref, kept, sums = refs[4], refs[5], refs[6:12], refs[12]
    rows = packed_ref.shape[0] // lc
    me_part = lax.axis_index(PART_AXES)
    for j in range(lc):
        backward_samples(n_cell, freq_count, codes_ref, w_out_ref[me_part * lc + j], [w[j] for w in weights],
                         arrived, sums if j else None, table_ref if j == lc - 1 else sums,
                         [k.at[j] for k in kept], j)
        sum_weights([k.at[j] for k in kept], packed_ref.at[j * rows:(j + 1) * rows])


def relay_kernel(tables_ref, packed_ref, _, out_ref):
    total = sum(tables_ref[k].astype(F32) for k in range(tables_ref.shape[0]))
    out_ref[0:packed_ref.shape[0], :] = packed_ref[...]
    out_ref[packed_ref.shape[0]:, :] = total.astype(BF16)


def unpack_kernel(places, lc, n_prev, packed_rows, tables_at, *refs):
    ins, refs = refs[:len(places)], refs[len(places):]
    if tables_at:
        here, refs = refs[0], refs[1:]
    outs, refs = refs[n_prev:n_prev + 4], refs[n_prev + 4:]
    code = outs[2].shape[1]
    if tables_at:
        cams = refs[0].shape[1]
        first = lc * packed_rows
        total = here[first:, :].astype(F32)
        for i in tables_at:
            total = total + ins[i][first:, :].astype(F32)
        total = jnp.concatenate([total[:, c:c + cams] for c in range(0, total.shape[1], cams)], axis=0)
        refs[0][...] = total[code:code + 3]
        refs[1][...] = total[0:code]
        refs = refs[2:]
    wide, sems = refs[:-1], refs[-1]
    enc_v, hidden_v, code_v, out_v = wide
    enc_rows, enc_cols = enc_v.shape[1:]
    hidden, color = hidden_v.shape[1:]
    out_rows = out_v.shape[1]
    me_part = lax.axis_index(PART_AXES)
    copies = []
    for i in range(len(places) * lc):
        cell = (me_part ^ places[i // lc]) * lc + i % lc
        src = ins[i // lc]
        row = i % lc * packed_rows
        for part in range(enc_cols // color):
            enc_v[i, :, part * color:(part + 1) * color] = src[row:row + enc_rows, :].astype(F32)
            row += enc_rows
        hidden_v[i] = src[row:row + hidden, :].astype(F32)
        row += hidden
        code_v[i] = src[row:row + code, :].astype(F32)
        row += code
        out_v[i] = src[row:row + RECORD, :].astype(F32)[TANGENT_ROW:TANGENT_ROW + out_rows]
        for m in range(4):
            copy = pltpu.make_async_copy(wide[m].at[i], outs[m].at[cell], sems.at[i, m])
            copy.start()
            copies.append(copy)
    for copy in copies:
        copy.wait()


def cost(us):
    return pl.CostEstimate(flops=us * 10 ** 9, bytes_accessed=us * 3 * 10 ** 6, transcendentals=0)


def exchange(value, axes, count, k):
    if k == 0:
        return value
    return lax.ppermute(value, axes, [(i, i ^ k) for i in range(count)])


def shards(points, cotangent, cell_ids, camera_ids, valid, w_enc, w_hidden, w_code, w_out, poses, codes):
    n_cell, n_rep, n_sub = lax.axis_size("cell"), lax.axis_size("rep"), lax.axis_size("sub")
    n_part = n_rep * n_sub
    local = w_enc.shape[0]
    lc = local // n_part
    cells_all = local * n_cell
    n = points.shape[1]
    cap = max(2, 2 * n // cells_all)
    enc, hidden = w_enc.shape[1:]
    color = w_hidden.shape[2]
    freq_count = enc // 8
    cams = poses.shape[1]
    code = codes.shape[0]
    width = n_part * cap
    params = pltpu.CompilerParams(vmem_limit_bytes=VMEM_BYTES)
    vmem = pl.BlockSpec(memory_space=pltpu.VMEM)
    hbm = pl.BlockSpec(memory_space=pltpu.HBM)

    inputs = (points, cotangent, cell_ids.reshape(1, n), camera_ids.reshape(1, n), valid.reshape(1, n), poses)
    weights = (w_enc, w_hidden, w_code)
    out_shape = [jax.ShapeDtypeStruct((cells_all * RECORD, cap), BF16)] + [
        jax.ShapeDtypeStruct((lc,) + w.shape[1:], BF16) for w in weights
    ]
    room = sum(2 * a.size // a.shape[-1] * max(a.shape[-1], 128) for a in out_shape) + SLACK_BYTES
    placed = pl.pallas_call(
        functools.partial(place_kernel, cells_all, cap, n_cell, n_part),
        out_shape=out_shape,
        in_specs=[hbm] * 9,
        out_specs=[vmem] * len(out_shape),
        scratch_shapes=[pltpu.VMEM(a.shape, a.dtype) for a in inputs] + [
            pltpu.VMEM((cells_all * RECORD, n), BF16),
            pltpu.SemaphoreType.DMA((9,)),
        ],
        compiler_params=pltpu.CompilerParams(vmem_limit_bytes=ALL_VMEM_BYTES - room),
        cost_estimate=cost(3),
        name="place",
    )(*inputs, *weights)
    sent, own_weights = placed[0], placed[1:]
    codes_cell = codes.reshape(code, n_cell, cams).transpose(1, 0, 2)
    w_out_rows = jnp.pad(w_out, ((0, 0), (TANGENT_ROW, RECORD - TANGENT_ROW - w_out.shape[1]), (0, 0)))

    arrived = lax.all_to_all(
        sent.reshape(n_cell * n_part, lc * RECORD, cap), ("cell",) + PART_AXES, 0, 0, tiled=True
    )
    if cap % 128:
        arrived = arrived.reshape(n_cell, n_part, lc * RECORD, cap).transpose(0, 2, 1, 3)
        arrived = arrived.reshape(n_cell, lc * RECORD, width)

    packed_rows = enc * (hidden // color) + hidden + code + RECORD
    slots = n_cell * width
    kept_rows = (enc, hidden, hidden + code, color, color, RECORD)
    table_shape = (n_cell, code + RECORD, cams)
    folded = (table_shape[1] * cams // color, color)
    packed, table = pl.pallas_call(
        functools.partial(cells_kernel, n_cell, freq_count, lc),
        in_specs=[vmem] * 6,
        out_specs=[vmem, vmem],
        out_shape=[
            jax.ShapeDtypeStruct((lc * packed_rows, color), BF16),
            jax.ShapeDtypeStruct((n_cell * n_rep,) + folded, BF16),
        ],
        scratch_shapes=[pltpu.VMEM((lc, r, slots), BF16) for r in kept_rows] + [pltpu.VMEM(table_shape, F32)],
        compiler_params=params,
        cost_estimate=cost(10),
        name="cells",
    )(codes_cell, w_out_rows, *own_weights, arrived)

    over_rep = [exchange(packed, "rep", n_rep, kr) for kr in range(n_rep)]
    over_sub = [exchange(packed, "sub", n_sub, ks) for ks in range(n_sub)]
    tables = lax.all_to_all(table, ("cell", "rep"), 0, 0, tiled=True)
    relayed = pl.pallas_call(
        relay_kernel,
        in_specs=[vmem] * 3,
        out_specs=vmem,
        out_shape=jax.ShapeDtypeStruct((lc * packed_rows + folded[0], color), BF16),
        compiler_params=params,
        cost_estimate=cost(0),
        name="relay",
    )(tables, over_rep[1], over_sub[-1])

    early, late = [], []
    for kr in range(n_rep):
        for ks in range(n_sub):
            if kr == 0:
                early.append((ks, over_sub[ks]))
            elif ks == 0:
                early.append((kr * n_sub, over_rep[kr]))
            else:
                sent_on = relayed if kr == 1 else over_rep[kr]
                late.append((kr * n_sub + ks, exchange(sent_on, "sub", n_sub, ks)))
    shapes = [
        jax.ShapeDtypeStruct((local, enc, hidden), F32),
        jax.ShapeDtypeStruct((local, hidden, color), F32),
        jax.ShapeDtypeStruct((local, code, color), F32),
        jax.ShapeDtypeStruct((local, w_out.shape[1], color), F32),
    ]
    grads = []
    for group in (early, late):
        tables_at, sums_shape, here = (), [], []
        if group is late:
            tables_at = tuple(i for i, (place, _) in enumerate(group) if place // n_sub == 1)
            sums_shape = [jax.ShapeDtypeStruct((rows, cams), F32) for rows in (3, code)]
            here = [relayed]
        grads = pl.pallas_call(
            functools.partial(
                unpack_kernel, tuple(place for place, _ in group), lc, len(grads), packed_rows, tables_at
            ),
            out_shape=shapes + sums_shape,
            in_specs=[vmem] * (len(group) + len(here)) + [hbm] * len(grads),
            out_specs=[hbm] * 4 + [vmem] * len(sums_shape),
            scratch_shapes=[pltpu.VMEM((len(group) * lc,) + a.shape[1:], F32) for a in shapes]
            + [pltpu.SemaphoreType.DMA((len(group) * lc, 4))],
            input_output_aliases={len(group) + len(here) + i: i for i in range(len(grads))},
            compiler_params=params,
            cost_estimate=cost(0),
            name="unpack",
        )(*[value for _, value in group], *here, *grads)
    return tuple(grads)


def solution(mesh):
    samples = ("groups", "cell", "rep", "sub")
    in_specs = (
        P(None, samples),
        P(None, samples),
        P(samples, None),
        P(samples),
        P(samples),
        P("cell", None, None),
        P("cell", None, None),
        P("cell", None, None),
        P("cell", None, None),
        P(None, "cell"),
        P(),
    )
    out_specs = (
        P(("groups", "cell"), None, None),
        P(("groups", "cell"), None, None),
        P(("groups", "cell"), None, None),
        P(("groups", "cell"), None, None),
        P(None, ("groups", "cell")),
        P(None, ("groups", "cell")),
    )
    return jax.shard_map(shards, mesh=mesh, in_specs=in_specs, out_specs=out_specs, check_vma=False)
```

```python
import functools

import jax
import jax.numpy as jnp
from jax import lax
from jax.experimental import pallas as pl
from jax.experimental.pallas import tpu as pltpu
from jax.sharding import PartitionSpec as P

BF16 = jnp.bfloat16
F32 = jnp.float32
VMEM_BYTES = 32 * 1024 * 1024
ALL_VMEM_BYTES = 64 * 1024 * 1024
SLACK_BYTES = 128 * 1024
PART_AXES = ("rep", "sub")
TOGETHER = 2
RECORD = 16
TANGENT_ROW = 8
CAMERA_ROW = 12


def dot_nn(a, b):
    return lax.dot_general(a, b, (((1,), (0,)), ((), ())), preferred_element_type=F32)


def dot_nt(a, b):
    return lax.dot_general(a, b, (((1,), (1,)), ((), ())), preferred_element_type=F32)


def dot_tn(a, b):
    return lax.dot_general(a, b, (((0,), (0,)), ((), ())), preferred_element_type=F32)


def iota(shape, dim):
    return lax.broadcasted_iota(jnp.int32, shape, dim)


def place_kernel(cells_all, cap, n_cell, n_part, *refs):
    sources, weights, placed, own = refs[:6], refs[6:9], refs[9], refs[10:13]
    arrays, (spread, sems) = refs[13:19], refs[19:]
    points_ref, cot_ref, cell_ref, cam_ref, valid_ref, poses_ref = arrays
    me_part = lax.axis_index(PART_AXES)
    lc = cells_all // (n_cell * n_part)
    pairs = list(zip(sources, arrays)) + [
        (source.at[pl.ds(me_part * lc, lc)], target) for source, target in zip(weights, own)
    ]
    copies = [pltpu.make_async_copy(source, target, sems.at[i]) for i, (source, target) in enumerate(pairs)]
    for copy in copies:
        copy.start()
    for copy in copies[:6]:
        copy.wait()
    n = points_ref.shape[1]
    cams = poses_ref.shape[1]
    cam = cam_ref[...]
    cam_hot = (iota((cams, n), 0) == cam).astype(F32).astype(BF16)
    poses = poses_ref[...]
    high = poses.astype(BF16).astype(F32)
    middle = (poses - high).astype(BF16).astype(F32)
    parts = jnp.concatenate([high, middle, poses - high - middle], axis=0).astype(BF16)
    moved = dot_nn(parts, cam_hot)
    offsets = (moved[0:3] + moved[3:6]) + moved[6:9]
    points = points_ref[...]
    coords = jnp.concatenate([points[0:3] + offsets, points[3:4]], axis=0)
    coords_high = coords.astype(BF16).astype(F32)
    tangent = cot_ref[...] * valid_ref[...].astype(F32)
    record = jnp.concatenate(
        [coords_high, coords - coords_high, tangent, cam.astype(F32), jnp.zeros((3, n), F32)], axis=0
    )
    width = min(256, n)
    blocks = n // width
    upper = (iota((width, width), 0) <= iota((width, width), 1)).astype(F32).astype(BF16)
    cell_of = cell_ref[...]
    hots = [
        (iota((cells_all, width), 0) == cell_of[:, b * width:(b + 1) * width]).astype(F32)
        for b in range(blocks)
    ]
    counts = dot_nn(jnp.concatenate(hots, axis=0).astype(BF16), upper)
    carry = jnp.zeros((cells_all, 1), F32)
    ranks = []
    for b in range(blocks):
        counted = counts[b * cells_all:(b + 1) * cells_all]
        ranks.append(jnp.sum((counted + carry) * hots[b], axis=0, keepdims=True) - 1.0)
        carry = carry + counted[:, width - 1:width]
    rank = jnp.concatenate(ranks, axis=1).astype(jnp.int32)
    rank_hot = (iota((cap, n), 0) == rank).astype(F32).astype(BF16)
    cell_rows = jnp.broadcast_to(cell_of, (RECORD, n))
    for c in range(cells_all):
        spread[c * RECORD:(c + 1) * RECORD, :] = jnp.where(cell_rows == c, record, 0.0).astype(BF16)
    placed[...] = dot_nt(spread[...], rank_hot).astype(BF16)
    for copy in copies[6:]:
        copy.wait()


def sin_cos(x):
    n = jnp.floor(x * 0.6366197723675814 + 0.5)
    r = ((x - n * 1.5703125) - n * 4.837512969970703125e-4) - n * 7.54978995489188216e-8
    z = r * r
    s = r + (r * z) * (-1.6666654611e-1 + z * (8.3321608736e-3 + z * -1.9515295891e-4))
    c = (1.0 - 0.5 * z) + (z * z) * (
        4.166664568298827e-2 + z * (-1.388731625493765e-3 + z * 2.443315711809948e-5))
    q = n.astype(jnp.int32)
    swap = (q & 1) == 1
    sine = jnp.where(swap, c, s)
    cosine = jnp.where(swap, s, c)
    sine = jnp.where((q & 2) == 2, -sine, sine)
    cosine = jnp.where(((q + 1) & 2) == 2, -cosine, cosine)
    return sine, cosine


def double_angle(s, c):
    return 2.0 * s * c, 1.0 - 2.0 * s * s


def soft(x):
    e = jnp.exp(-jnp.abs(x))
    u = 1.0 + e
    plus = jnp.maximum(x, 0.0) + jnp.where(e < 1e-4, e, jnp.log(u))
    r = pl.reciprocal(u, approx=True)
    return plus, jnp.where(x >= 0.0, r, e * r)


def fold(table, rows):
    return jnp.concatenate([table[r:r + rows] for r in range(0, table.shape[0], rows)], axis=1)


def chunk_steps(freq_count, kc, cols, rec, weights, code_part, w_out_t, kept, results):
    enc_s, gt_s, trunk_s, gc_s, act_s, rec_s = kept
    w_enc, w_enc_t, w_hidden, w_hidden_t = weights
    cams = code_part.shape[1] // 2
    width = rec.shape[1]
    half = freq_count // 2
    scale = jnp.exp2(iota((half, 1), 0).astype(F32) * 0.25)
    top = 2.0 ** (half // 4)
    rec_s[:, cols] = rec
    recf = rec.astype(F32)
    coords = recf[0:4] + recf[4:8]
    cam = recf[CAMERA_ROW:CAMERA_ROW + 1].astype(jnp.int32)
    cam_hot = (iota((cams, width), 0) == cam).astype(F32).astype(BF16)
    angles = jnp.concatenate([coords[i:i + 1] * scale for i in range(4)], axis=0)
    s1, c1 = sin_cos(angles)
    s2, c2 = s1, c1
    for _ in range(half // 4):
        s2, c2 = double_angle(s2, c2)
    pieces = []
    for a, b in ((s1, s2), (c1, c2)):
        for i in range(4):
            pieces += [a[i * half:(i + 1) * half], b[i * half:(i + 1) * half]]
    encoded = jnp.concatenate(pieces, axis=0).astype(BF16)
    enc_s[:, cols] = encoded
    yield
    trunk, slope_trunk = soft(dot_nn(w_enc_t, encoded))
    trunk = trunk.astype(BF16)
    trunk_s[:, cols] = trunk
    yield
    act, slope_color = soft(
        dot_nn(w_hidden_t, trunk) + dot_nn(code_part, jnp.concatenate([cam_hot, cam_hot], axis=0))
    )
    act_s[:, cols] = act.astype(BF16)
    gc = (dot_nn(w_out_t, rec) * slope_color).astype(BF16)
    gc_s[:, cols] = gc
    yield
    gt = (dot_nn(w_hidden, gc) * slope_trunk).astype(BF16)
    gt_s[:, cols] = gt
    camera_color = dot_nt(cam_hot, gc)
    yield
    grad_enc = dot_nn(w_enc, gt)
    sums = []
    for i in range(3):
        a, b = i * 2 * half, (4 + i) * 2 * half
        at = slice(i * half, (i + 1) * half)
        first = grad_enc[a:a + half] * c1[at] - grad_enc[b:b + half] * s1[at]
        second = grad_enc[a + half:a + 2 * half] * c2[at] - grad_enc[b + half:b + 2 * half] * s2[at]
        sums.append(jnp.sum((first + top * second) * scale, axis=0, keepdims=True))
    row = iota((RECORD, width), 0)
    tail = jnp.where(row == 0, sums[0], jnp.where(row == 1, sums[1], jnp.where(row == 2, sums[2], 0.0)))
    results[kc] = (camera_color.astype(BF16), dot_nt(tail.astype(BF16), cam_hot))


def cells_kernel(n_cell, freq_count, lc, codes_ref, w_out_ref, *refs):
    weights_refs, arrived = refs[:3], refs[3]
    packed_ref, table_ref, kept_refs, sums = refs[4], refs[5], refs[6:12], refs[12]
    rows = packed_ref.shape[0] // lc
    blocks = arrived.shape[0] // n_cell
    width = blocks * arrived.shape[2]
    cams = codes_ref.shape[1] // n_cell
    me_part = lax.axis_index(PART_AXES)
    codes = codes_ref[...]
    for j in range(lc):
        kept = [k.at[j] for k in kept_refs]
        enc_s, gt_s, trunk_s, gc_s, act_s, rec_s = kept
        w_enc, w_hidden, w_code = (w[j] for w in weights_refs)
        w_out_t = w_out_ref[me_part * lc + j].T
        weights = (w_enc, w_enc.T, w_hidden, w_hidden.T)
        coded = dot_tn(w_code, codes)
        coded_high = coded.astype(BF16)
        coded_low = (coded - coded_high.astype(F32)).astype(BF16)
        results = [None] * n_cell
        steps = []
        for kc in range(n_cell):
            rec = jnp.concatenate(
                [arrived[kc * blocks + b, j * RECORD:(j + 1) * RECORD, :] for b in range(blocks)], axis=1
            )
            at = slice(kc * cams, (kc + 1) * cams)
            code_part = jnp.concatenate([coded_high[:, at], coded_low[:, at]], axis=1)
            cols = slice(kc * width, (kc + 1) * width)
            steps.append(
                chunk_steps(freq_count, kc, cols, rec, weights, code_part, w_out_t, kept, results)
            )
        for first in range(0, n_cell, TOGETHER):
            live = steps[first:first + TOGETHER]
            while live:
                live = [step for step in live if next(step, live) is not live]
        for kc in range(n_cell):
            camera_color, camera_pose = results[kc]
            table = jnp.concatenate([dot_nt(w_code, camera_color), camera_pose], axis=0)
            if j:
                table = table + sums[kc]
            if j < lc - 1:
                sums[kc] = table
            else:
                copies = table_ref.shape[0] // n_cell
                for i in range(copies):
                    table_ref[kc * copies + i] = fold(table, table_ref.shape[1]).astype(BF16)
        row = j * rows
        color = gc_s.shape[0]
        g_enc = dot_nt(enc_s[...], gt_s[...]).astype(BF16)
        for part in range(g_enc.shape[1] // color):
            packed_ref[row:row + g_enc.shape[0], :] = g_enc[:, part * color:(part + 1) * color]
            row += g_enc.shape[0]
        hidden, code = trunk_s.shape[0], codes.shape[0]
        packed_ref[row:row + hidden, :] = dot_nt(trunk_s[...], gc_s[...]).astype(BF16)
        row += hidden
        camera_color = jnp.concatenate([result[0] for result in results], axis=0)
        packed_ref[row:row + code, :] = dot_nn(codes, camera_color).astype(BF16)
        row += code
        packed_ref[row:row + RECORD, :] = dot_nt(rec_s[...], act_s[...]).astype(BF16)


def relay_kernel(tables_ref, packed_ref, _, out_ref):
    total = sum(tables_ref[k].astype(F32) for k in range(tables_ref.shape[0]))
    out_ref[0:packed_ref.shape[0], :] = packed_ref[...]
    out_ref[packed_ref.shape[0]:, :] = total.astype(BF16)


def unpack_kernel(places, lc, n_prev, packed_rows, tables_at, *refs):
    ins, refs = refs[:len(places)], refs[len(places):]
    if tables_at:
        here, refs = refs[0], refs[1:]
    outs, refs = refs[n_prev:n_prev + 4], refs[n_prev + 4:]
    code = outs[2].shape[1]
    if tables_at:
        cams = refs[0].shape[1]
        first = lc * packed_rows
        total = here[first:, :].astype(F32)
        for i in tables_at:
            total = total + ins[i][first:, :].astype(F32)
        total = jnp.concatenate([total[:, c:c + cams] for c in range(0, total.shape[1], cams)], axis=0)
        refs[0][...] = total[code:code + 3]
        refs[1][...] = total[0:code]
        refs = refs[2:]
    wide, sems = refs[:-1], refs[-1]
    enc_v, hidden_v, code_v, out_v = wide
    enc_rows, enc_cols = enc_v.shape[1:]
    hidden, color = hidden_v.shape[1:]
    out_rows = out_v.shape[1]
    me_part = lax.axis_index(PART_AXES)
    copies = []
    for i in range(len(places) * lc):
        cell = (me_part ^ places[i // lc]) * lc + i % lc
        src = ins[i // lc]
        row = i % lc * packed_rows
        for part in range(enc_cols // color):
            enc_v[i, :, part * color:(part + 1) * color] = src[row:row + enc_rows, :].astype(F32)
            row += enc_rows
        hidden_v[i] = src[row:row + hidden, :].astype(F32)
        row += hidden
        code_v[i] = src[row:row + code, :].astype(F32)
        row += code
        out_v[i] = src[row:row + RECORD, :].astype(F32)[TANGENT_ROW:TANGENT_ROW + out_rows]
        for m in range(4):
            copy = pltpu.make_async_copy(wide[m].at[i], outs[m].at[cell], sems.at[i, m])
            copy.start()
            copies.append(copy)
    for copy in copies:
        copy.wait()


def cost(us):
    return pl.CostEstimate(flops=us * 10 ** 9, bytes_accessed=us * 3 * 10 ** 6, transcendentals=0)


def exchange(value, axes, count, k):
    if k == 0:
        return value
    return lax.ppermute(value, axes, [(i, i ^ k) for i in range(count)])


def shards(points, cotangent, cell_ids, camera_ids, valid, w_enc, w_hidden, w_code, w_out, poses, codes):
    n_cell, n_rep, n_sub = lax.axis_size("cell"), lax.axis_size("rep"), lax.axis_size("sub")
    n_part = n_rep * n_sub
    local = w_enc.shape[0]
    lc = local // n_part
    cells_all = local * n_cell
    n = points.shape[1]
    cap = max(2, 2 * n // cells_all)
    enc, hidden = w_enc.shape[1:]
    color = w_hidden.shape[2]
    freq_count = enc // 8
    cams = poses.shape[1]
    code = codes.shape[0]
    width = n_part * cap
    params = pltpu.CompilerParams(vmem_limit_bytes=VMEM_BYTES)
    vmem = pl.BlockSpec(memory_space=pltpu.VMEM)
    hbm = pl.BlockSpec(memory_space=pltpu.HBM)

    inputs = (points, cotangent, cell_ids.reshape(1, n), camera_ids.reshape(1, n), valid.reshape(1, n), poses)
    weights = (w_enc, w_hidden, w_code)
    out_shape = [jax.ShapeDtypeStruct((cells_all * RECORD, cap), BF16)] + [
        jax.ShapeDtypeStruct((lc,) + w.shape[1:], BF16) for w in weights
    ]
    room = sum(2 * a.size // a.shape[-1] * max(a.shape[-1], 128) for a in out_shape) + SLACK_BYTES
    placed = pl.pallas_call(
        functools.partial(place_kernel, cells_all, cap, n_cell, n_part),
        out_shape=out_shape,
        in_specs=[hbm] * 9,
        out_specs=[vmem] * len(out_shape),
        scratch_shapes=[pltpu.VMEM(a.shape, a.dtype) for a in inputs] + [
            pltpu.VMEM((cells_all * RECORD, n), BF16),
            pltpu.SemaphoreType.DMA((9,)),
        ],
        compiler_params=pltpu.CompilerParams(vmem_limit_bytes=ALL_VMEM_BYTES - room),
        cost_estimate=cost(3),
        name="place",
    )(*inputs, *weights)
    sent, own_weights = placed[0], placed[1:]
    w_out_rows = jnp.pad(w_out, ((0, 0), (TANGENT_ROW, RECORD - TANGENT_ROW - w_out.shape[1]), (0, 0)))

    arrived = lax.all_to_all(
        sent.reshape(n_cell * n_part, lc * RECORD, cap), ("cell",) + PART_AXES, 0, 0, tiled=True
    )
    if cap % 128:
        arrived = arrived.reshape(n_cell, n_part, lc * RECORD, cap).transpose(0, 2, 1, 3)
        arrived = arrived.reshape(n_cell, lc * RECORD, width)

    packed_rows = enc * (hidden // color) + hidden + code + RECORD
    slots = n_cell * width
    kept_rows = (enc, hidden, hidden, color, color, RECORD)
    table_shape = (n_cell, code + RECORD, cams)
    folded = (table_shape[1] * cams // color, color)
    packed, table = pl.pallas_call(
        functools.partial(cells_kernel, n_cell, freq_count, lc),
        in_specs=[vmem] * 6,
        out_specs=[vmem, vmem],
        out_shape=[
            jax.ShapeDtypeStruct((lc * packed_rows, color), BF16),
            jax.ShapeDtypeStruct((n_cell * n_rep,) + folded, BF16),
        ],
        scratch_shapes=[pltpu.VMEM((lc, r, slots), BF16) for r in kept_rows] + [pltpu.VMEM(table_shape, F32)],
        compiler_params=params,
        cost_estimate=cost(10),
        name="cells",
    )(codes, w_out_rows, *own_weights, arrived)

    over_rep = [exchange(packed, "rep", n_rep, kr) for kr in range(n_rep)]
    over_sub = [exchange(packed, "sub", n_sub, ks) for ks in range(n_sub)]
    tables = lax.all_to_all(table, ("cell", "rep"), 0, 0, tiled=True)
    relayed = pl.pallas_call(
        relay_kernel,
        in_specs=[vmem] * 3,
        out_specs=vmem,
        out_shape=jax.ShapeDtypeStruct((lc * packed_rows + folded[0], color), BF16),
        compiler_params=params,
        cost_estimate=cost(0),
        name="relay",
    )(tables, over_rep[1], over_sub[-1])

    early, late = [], []
    for kr in range(n_rep):
        for ks in range(n_sub):
            if kr == 0:
                early.append((ks, over_sub[ks]))
            elif ks == 0:
                early.append((kr * n_sub, over_rep[kr]))
            else:
                sent_on = relayed if kr == 1 else over_rep[kr]
                late.append((kr * n_sub + ks, exchange(sent_on, "sub", n_sub, ks)))
    shapes = [
        jax.ShapeDtypeStruct((local, enc, hidden), F32),
        jax.ShapeDtypeStruct((local, hidden, color), F32),
        jax.ShapeDtypeStruct((local, code, color), F32),
        jax.ShapeDtypeStruct((local, w_out.shape[1], color), F32),
    ]
    grads = []
    for group in (early, late):
        tables_at, sums_shape, here = (), [], []
        if group is late:
            tables_at = tuple(i for i, (place, _) in enumerate(group) if place // n_sub == 1)
            sums_shape = [jax.ShapeDtypeStruct((rows, cams), F32) for rows in (3, code)]
            here = [relayed]
        grads = pl.pallas_call(
            functools.partial(
                unpack_kernel, tuple(place for place, _ in group), lc, len(grads), packed_rows, tables_at
            ),
            out_shape=shapes + sums_shape,
            in_specs=[vmem] * (len(group) + len(here)) + [hbm] * len(grads),
            out_specs=[hbm] * 4 + [vmem] * len(sums_shape),
            scratch_shapes=[pltpu.VMEM((len(group) * lc,) + a.shape[1:], F32) for a in shapes]
            + [pltpu.SemaphoreType.DMA((len(group) * lc, 4))],
            input_output_aliases={len(group) + len(here) + i: i for i in range(len(grads))},
            compiler_params=params,
            cost_estimate=cost(0),
            name="unpack",
        )(*[value for _, value in group], *here, *grads)
    return tuple(grads)


def solution(mesh):
    samples = ("groups", "cell", "rep", "sub")
    in_specs = (
        P(None, samples),
        P(None, samples),
        P(samples, None),
        P(samples),
        P(samples),
        P("cell", None, None),
        P("cell", None, None),
        P("cell", None, None),
        P("cell", None, None),
        P(None, "cell"),
        P(),
    )
    out_specs = (
        P(("groups", "cell"), None, None),
        P(("groups", "cell"), None, None),
        P(("groups", "cell"), None, None),
        P(("groups", "cell"), None, None),
        P(None, ("groups", "cell")),
        P(None, ("groups", "cell")),
    )
    return jax.shard_map(shards, mesh=mesh, in_specs=in_specs, out_specs=out_specs, check_vma=False)
```

```python
import functools

import jax
import jax.numpy as jnp
from jax import lax
from jax.experimental import pallas as pl
from jax.experimental.pallas import tpu as pltpu
from jax.sharding import PartitionSpec as P

BF16 = jnp.bfloat16
F32 = jnp.float32
VMEM_BYTES = 32 * 1024 * 1024
ALL_VMEM_BYTES = 64 * 1024 * 1024
SLACK_BYTES = 128 * 1024
PART_AXES = ("rep", "sub")
TOGETHER = 2
RECORD = 16
TANGENT_ROW = 8
CAMERA_ROW = 12


def dot_nn(a, b):
    return lax.dot_general(a, b, (((1,), (0,)), ((), ())), preferred_element_type=F32)


def dot_nt(a, b):
    return lax.dot_general(a, b, (((1,), (1,)), ((), ())), preferred_element_type=F32)


def dot_tn(a, b):
    return lax.dot_general(a, b, (((0,), (0,)), ((), ())), preferred_element_type=F32)


def iota(shape, dim):
    return lax.broadcasted_iota(jnp.int32, shape, dim)


def place_kernel(cells_all, cap, n_cell, n_part, *refs):
    sources, weights, placed, own = refs[:6], refs[6:9], refs[9], refs[10:13]
    arrays, (spread, sems) = refs[13:19], refs[19:]
    points_ref, cot_ref, cell_ref, cam_ref, valid_ref, poses_ref = arrays
    me_part = lax.axis_index(PART_AXES)
    lc = cells_all // (n_cell * n_part)
    pairs = list(zip(sources, arrays)) + [
        (source.at[pl.ds(me_part * lc, lc)], target) for source, target in zip(weights, own)
    ]
    copies = [pltpu.make_async_copy(source, target, sems.at[i]) for i, (source, target) in enumerate(pairs)]
    for copy in copies:
        copy.start()
    for copy in copies[:6]:
        copy.wait()
    n = points_ref.shape[1]
    cams = poses_ref.shape[1]
    cam = cam_ref[...]
    cam_hot = (iota((cams, n), 0) == cam).astype(F32).astype(BF16)
    poses = poses_ref[...]
    high = poses.astype(BF16).astype(F32)
    middle = (poses - high).astype(BF16).astype(F32)
    parts = jnp.concatenate([high, middle, poses - high - middle], axis=0).astype(BF16)
    moved = dot_nn(parts, cam_hot)
    offsets = (moved[0:3] + moved[3:6]) + moved[6:9]
    points = points_ref[...]
    coords = jnp.concatenate([points[0:3] + offsets, points[3:4]], axis=0)
    coords_high = coords.astype(BF16).astype(F32)
    tangent = cot_ref[...] * valid_ref[...].astype(F32)
    record = jnp.concatenate(
        [coords_high, coords - coords_high, tangent, cam.astype(F32), jnp.zeros((3, n), F32)], axis=0
    )
    width = min(256, n)
    blocks = n // width
    upper = (iota((width, width), 0) <= iota((width, width), 1)).astype(F32).astype(BF16)
    cell_of = cell_ref[...]
    hots = [
        (iota((cells_all, width), 0) == cell_of[:, b * width:(b + 1) * width]).astype(F32)
        for b in range(blocks)
    ]
    counts = dot_nn(jnp.concatenate(hots, axis=0).astype(BF16), upper)
    carry = jnp.zeros((cells_all, 1), F32)
    ranks = []
    for b in range(blocks):
        counted = counts[b * cells_all:(b + 1) * cells_all]
        ranks.append(jnp.sum((counted + carry) * hots[b], axis=0, keepdims=True) - 1.0)
        carry = carry + counted[:, width - 1:width]
    rank = jnp.concatenate(ranks, axis=1).astype(jnp.int32)
    rank_hot = (iota((cap, n), 0) == rank).astype(F32).astype(BF16)
    cell_rows = jnp.broadcast_to(cell_of, (RECORD, n))
    for c in range(cells_all):
        owner_cell, owner_part, j = c // (n_part * lc), c // lc % n_part, c % lc
        slot = (owner_part * n_cell + owner_cell) * lc + j
        spread[slot * RECORD:(slot + 1) * RECORD, :] = jnp.where(cell_rows == c, record, 0.0).astype(BF16)
    placed[...] = dot_nt(spread[...], rank_hot).astype(BF16)
    for copy in copies[6:]:
        copy.wait()


def sin_cos(x):
    n = jnp.floor(x * 0.6366197723675814 + 0.5)
    r = ((x - n * 1.5703125) - n * 4.837512969970703125e-4) - n * 7.54978995489188216e-8
    z = r * r
    s = r + (r * z) * (-1.6666654611e-1 + z * (8.3321608736e-3 + z * -1.9515295891e-4))
    c = (1.0 - 0.5 * z) + (z * z) * (
        4.166664568298827e-2 + z * (-1.388731625493765e-3 + z * 2.443315711809948e-5))
    q = n.astype(jnp.int32)
    swap = (q & 1) == 1
    sine = jnp.where(swap, c, s)
    cosine = jnp.where(swap, s, c)
    sine = jnp.where((q & 2) == 2, -sine, sine)
    cosine = jnp.where(((q + 1) & 2) == 2, -cosine, cosine)
    return sine, cosine


def double_angle(s, c):
    return 2.0 * s * c, 1.0 - 2.0 * s * s


def soft(x):
    e = jnp.exp(-jnp.abs(x))
    u = 1.0 + e
    plus = jnp.maximum(x, 0.0) + jnp.where(e < 1e-4, e, jnp.log(u))
    r = pl.reciprocal(u, approx=True)
    return plus, jnp.where(x >= 0.0, r, e * r)


def fold(table, rows):
    return jnp.concatenate([table[r:r + rows] for r in range(0, table.shape[0], rows)], axis=1)


def chunk_steps(freq_count, kc, cols, rec, weights, code_part, w_out_t, kept, results):
    enc_s, gt_s, trunk_s, gc_s, act_s, rec_s = kept
    w_enc, w_enc_t, w_hidden, w_hidden_t = weights
    cams = code_part.shape[1] // 2
    width = rec.shape[1]
    half = freq_count // 2
    scale = jnp.exp2(iota((half, 1), 0).astype(F32) * 0.25)
    top = 2.0 ** (half // 4)
    rec_s[:, cols] = rec
    recf = rec.astype(F32)
    coords = recf[0:4] + recf[4:8]
    cam = recf[CAMERA_ROW:CAMERA_ROW + 1].astype(jnp.int32)
    cam_hot = (iota((cams, width), 0) == cam).astype(F32).astype(BF16)
    angles = jnp.concatenate([coords[i:i + 1] * scale for i in range(4)], axis=0)
    s1, c1 = sin_cos(angles)
    s2, c2 = s1, c1
    for _ in range(half // 4):
        s2, c2 = double_angle(s2, c2)
    pieces = []
    for a, b in ((s1, s2), (c1, c2)):
        for i in range(4):
            pieces += [a[i * half:(i + 1) * half], b[i * half:(i + 1) * half]]
    encoded = jnp.concatenate(pieces, axis=0).astype(BF16)
    enc_s[:, cols] = encoded
    yield
    trunk, slope_trunk = soft(dot_nn(w_enc_t, encoded))
    trunk = trunk.astype(BF16)
    trunk_s[:, cols] = trunk
    yield
    act, slope_color = soft(
        dot_nn(w_hidden_t, trunk) + dot_nn(code_part, jnp.concatenate([cam_hot, cam_hot], axis=0))
    )
    act_s[:, cols] = act.astype(BF16)
    gc = (dot_nn(w_out_t, rec) * slope_color).astype(BF16)
    gc_s[:, cols] = gc
    yield
    gt = (dot_nn(w_hidden, gc) * slope_trunk).astype(BF16)
    gt_s[:, cols] = gt
    camera_color = dot_nt(cam_hot, gc)
    yield
    grad_enc = dot_nn(w_enc, gt)
    sums = []
    for i in range(3):
        a, b = i * 2 * half, (4 + i) * 2 * half
        at = slice(i * half, (i + 1) * half)
        first = grad_enc[a:a + half] * c1[at] - grad_enc[b:b + half] * s1[at]
        second = grad_enc[a + half:a + 2 * half] * c2[at] - grad_enc[b + half:b + 2 * half] * s2[at]
        sums.append(jnp.sum((first + top * second) * scale, axis=0, keepdims=True))
    row = iota((RECORD, width), 0)
    tail = jnp.where(row == 0, sums[0], jnp.where(row == 1, sums[1], jnp.where(row == 2, sums[2], 0.0)))
    results[kc] = (camera_color.astype(BF16), dot_nt(tail.astype(BF16), cam_hot))


def prepare_kernel(n_cell, codes_ref, w_out_ref, w_enc_ref, w_hidden_ref, w_code_ref,
                   w_enc_t_ref, w_hidden_t_ref, w_out_t_ref, coded_ref):
    me_part = lax.axis_index(PART_AXES)
    lc = w_enc_ref.shape[0]
    cams = codes_ref.shape[1] // n_cell
    for j in range(lc):
        w_enc_t_ref[j] = w_enc_ref[j].T
        w_hidden_t_ref[j] = w_hidden_ref[j].T
        w_out_t_ref[j] = w_out_ref[me_part * lc + j].T
        coded = dot_tn(w_code_ref[j], codes_ref[...])
        high = coded.astype(BF16)
        low = (coded - high.astype(F32)).astype(BF16)
        for kc in range(n_cell):
            at = slice(kc * cams, (kc + 1) * cams)
            coded_ref[j, kc] = jnp.concatenate([high[:, at], low[:, at]], axis=1)


def cells_kernel(n_cell, freq_count, lc, codes_ref, *refs):
    weights_refs, turned_refs, arrived = refs[:3], refs[3:7], refs[7]
    packed_ref, table_ref, kept_refs, sums = refs[8], refs[9], refs[10:16], refs[16]
    rows = packed_ref.shape[0] // lc
    blocks = arrived.shape[0] // n_cell
    width = blocks * arrived.shape[2]
    codes = codes_ref[...]
    for j in range(lc):
        kept = [k.at[j] for k in kept_refs]
        enc_s, gt_s, trunk_s, gc_s, act_s, rec_s = kept
        w_enc, w_hidden, w_code = (w[j] for w in weights_refs)
        w_enc_t, w_hidden_t, w_out_t, coded = (w.at[j] for w in turned_refs)
        w_out_t = w_out_t[...]
        weights = (w_enc, w_enc_t[...], w_hidden, w_hidden_t[...])
        results = [None] * n_cell
        steps = []
        for kc in range(n_cell):
            rec = jnp.concatenate(
                [arrived[b * n_cell + kc, j * RECORD:(j + 1) * RECORD, :] for b in range(blocks)], axis=1
            )
            cols = slice(kc * width, (kc + 1) * width)
            steps.append(
                chunk_steps(freq_count, kc, cols, rec, weights, coded[kc], w_out_t, kept, results)
            )
        for first in range(0, n_cell, TOGETHER):
            live = steps[first:first + TOGETHER]
            while live:
                live = [step for step in live if next(step, live) is not live]
        for kc in range(n_cell):
            camera_color, camera_pose = results[kc]
            table = jnp.concatenate([dot_nt(w_code, camera_color), camera_pose], axis=0)
            if j:
                table = table + sums[kc]
            if j < lc - 1:
                sums[kc] = table
            else:
                copies = table_ref.shape[0] // n_cell
                for i in range(copies):
                    table_ref[kc * copies + i] = fold(table, table_ref.shape[1]).astype(BF16)
        row = j * rows
        color = gc_s.shape[0]
        g_enc = dot_nt(enc_s[...], gt_s[...]).astype(BF16)
        for part in range(g_enc.shape[1] // color):
            packed_ref[row:row + g_enc.shape[0], :] = g_enc[:, part * color:(part + 1) * color]
            row += g_enc.shape[0]
        hidden, code = trunk_s.shape[0], codes.shape[0]
        packed_ref[row:row + hidden, :] = dot_nt(trunk_s[...], gc_s[...]).astype(BF16)
        row += hidden
        camera_color = jnp.concatenate([result[0] for result in results], axis=0)
        packed_ref[row:row + code, :] = dot_nn(codes, camera_color).astype(BF16)
        row += code
        packed_ref[row:row + RECORD, :] = dot_nt(rec_s[...], act_s[...]).astype(BF16)


def relay_kernel(tables_ref, packed_ref, _, out_ref):
    total = sum(tables_ref[k].astype(F32) for k in range(tables_ref.shape[0]))
    out_ref[0:packed_ref.shape[0], :] = packed_ref[...]
    out_ref[packed_ref.shape[0]:, :] = total.astype(BF16)


def unpack_kernel(places, lc, n_prev, packed_rows, tables_at, *refs):
    ins, refs = refs[:len(places)], refs[len(places):]
    if tables_at:
        here, refs = refs[0], refs[1:]
    outs, refs = refs[n_prev:n_prev + 4], refs[n_prev + 4:]
    camera_outs, refs = (refs[:2], refs[2:]) if tables_at else ((), refs)
    wide, sems = refs[:-1], refs[-1]
    enc_v, hidden_v, code_v, out_v = wide
    enc_rows, enc_cols = enc_v.shape[1:]
    hidden, color = hidden_v.shape[1:]
    code, out_rows = code_v.shape[1], out_v.shape[1]
    me_part = lax.axis_index(PART_AXES)
    copies = []
    for i in range(len(places) * lc):
        cell = (me_part ^ places[i // lc]) * lc + i % lc
        src = ins[i // lc]
        row = i % lc * packed_rows

        def send(m):
            copy = pltpu.make_async_copy(wide[m].at[i], outs[m].at[cell], sems.at[i, m])
            copy.start()
            copies.append(copy)

        for part in range(enc_cols // color):
            enc_v[i, :, part * color:(part + 1) * color] = src[row:row + enc_rows, :].astype(F32)
            row += enc_rows
        send(0)
        hidden_v[i] = src[row:row + hidden, :].astype(F32)
        row += hidden
        send(1)
        code_v[i] = src[row:row + code, :].astype(F32)
        row += code
        out_v[i] = src[row:row + RECORD, :].astype(F32)[TANGENT_ROW:TANGENT_ROW + out_rows]
        send(2)
        send(3)
    if tables_at:
        cams = camera_outs[0].shape[1]
        first = lc * packed_rows
        total = here[first:, :].astype(F32)
        for i in tables_at:
            total = total + ins[i][first:, :].astype(F32)
        total = jnp.concatenate([total[:, c:c + cams] for c in range(0, total.shape[1], cams)], axis=0)
        camera_outs[0][...] = total[code:code + 3]
        camera_outs[1][...] = total[0:code]
    for copy in copies:
        copy.wait()


def cost(us):
    return pl.CostEstimate(flops=us * 10 ** 9, bytes_accessed=us * 3 * 10 ** 6, transcendentals=0)


def exchange(value, axes, count, k):
    if k == 0:
        return value
    return lax.ppermute(value, axes, [(i, i ^ k) for i in range(count)])


def shards(points, cotangent, cell_ids, camera_ids, valid, w_enc, w_hidden, w_code, w_out, poses, codes):
    n_cell, n_rep, n_sub = lax.axis_size("cell"), lax.axis_size("rep"), lax.axis_size("sub")
    n_part = n_rep * n_sub
    local = w_enc.shape[0]
    lc = local // n_part
    cells_all = local * n_cell
    n = points.shape[1]
    cap = max(2, 2 * n // cells_all)
    enc, hidden = w_enc.shape[1:]
    color = w_hidden.shape[2]
    freq_count = enc // 8
    cams = poses.shape[1]
    code = codes.shape[0]
    width = n_part * cap
    params = pltpu.CompilerParams(vmem_limit_bytes=VMEM_BYTES)
    vmem = pl.BlockSpec(memory_space=pltpu.VMEM)
    hbm = pl.BlockSpec(memory_space=pltpu.HBM)

    inputs = (points, cotangent, cell_ids.reshape(1, n), camera_ids.reshape(1, n), valid.reshape(1, n), poses)
    weights = (w_enc, w_hidden, w_code)
    out_shape = [jax.ShapeDtypeStruct((cells_all * RECORD, cap), BF16)] + [
        jax.ShapeDtypeStruct((lc,) + w.shape[1:], BF16) for w in weights
    ]
    room = sum(2 * a.size // a.shape[-1] * max(a.shape[-1], 128) for a in out_shape) + SLACK_BYTES
    placed = pl.pallas_call(
        functools.partial(place_kernel, cells_all, cap, n_cell, n_part),
        out_shape=out_shape,
        in_specs=[hbm] * 9,
        out_specs=[vmem] * len(out_shape),
        scratch_shapes=[pltpu.VMEM(a.shape, a.dtype) for a in inputs] + [
            pltpu.VMEM((cells_all * RECORD, n), BF16),
            pltpu.SemaphoreType.DMA((9,)),
        ],
        compiler_params=pltpu.CompilerParams(vmem_limit_bytes=ALL_VMEM_BYTES - room),
        cost_estimate=cost(3),
        name="place",
    )(*inputs, *weights)
    sent, own_weights = placed[0], placed[1:]
    w_out_rows = jnp.pad(w_out, ((0, 0), (TANGENT_ROW, RECORD - TANGENT_ROW - w_out.shape[1]), (0, 0)))

    arrived = lax.all_to_all(
        sent.reshape(n_cell * n_part, lc * RECORD, cap), PART_AXES + ("cell",), 0, 0, tiled=True
    )
    if cap % 128:
        arrived = arrived.reshape(n_part, n_cell, lc * RECORD, cap).transpose(1, 2, 0, 3)
        arrived = arrived.reshape(n_cell, lc * RECORD, width)

    packed_rows = enc * (hidden // color) + hidden + code + RECORD
    slots = n_cell * width
    kept_rows = (enc, hidden, hidden, color, color, RECORD)
    table_shape = (n_cell, code + RECORD, cams)
    folded = (table_shape[1] * cams // color, color)
    turned = pl.pallas_call(
        functools.partial(prepare_kernel, n_cell),
        in_specs=[vmem] * 5,
        out_specs=[vmem] * 4,
        out_shape=[
            jax.ShapeDtypeStruct((lc, hidden, enc), BF16),
            jax.ShapeDtypeStruct((lc, color, hidden), BF16),
            jax.ShapeDtypeStruct((lc, color, RECORD), BF16),
            jax.ShapeDtypeStruct((lc, n_cell, color, 2 * cams), BF16),
        ],
        compiler_params=params,
        cost_estimate=cost(2),
        name="prepare",
    )(codes, w_out_rows, *own_weights)
    packed, table = pl.pallas_call(
        functools.partial(cells_kernel, n_cell, freq_count, lc),
        in_specs=[vmem] * 9,
        out_specs=[vmem, vmem],
        out_shape=[
            jax.ShapeDtypeStruct((lc * packed_rows, color), BF16),
            jax.ShapeDtypeStruct((n_cell * n_rep,) + folded, BF16),
        ],
        scratch_shapes=[pltpu.VMEM((lc, r, slots), BF16) for r in kept_rows] + [pltpu.VMEM(table_shape, F32)],
        compiler_params=params,
        cost_estimate=cost(10),
        name="cells",
    )(codes, *own_weights, *turned, arrived)

    over_rep = [exchange(packed, "rep", n_rep, kr) for kr in range(n_rep)]
    over_sub = [exchange(packed, "sub", n_sub, ks) for ks in range(n_sub)]
    tables = lax.all_to_all(table, ("cell", "rep"), 0, 0, tiled=True)
    relayed = pl.pallas_call(
        relay_kernel,
        in_specs=[vmem] * 3,
        out_specs=vmem,
        out_shape=jax.ShapeDtypeStruct((lc * packed_rows + folded[0], color), BF16),
        compiler_params=params,
        cost_estimate=cost(0),
        name="relay",
    )(tables, over_rep[1], over_sub[-1])

    early, late = [], []
    for kr in range(n_rep):
        for ks in range(n_sub):
            if kr == 0:
                early.append((ks, over_sub[ks]))
            elif ks == 0:
                early.append((kr * n_sub, over_rep[kr]))
            else:
                sent_on = relayed if kr == 1 else over_rep[kr]
                late.append((kr * n_sub + ks, exchange(sent_on, "sub", n_sub, ks)))
    shapes = [
        jax.ShapeDtypeStruct((local, enc, hidden), F32),
        jax.ShapeDtypeStruct((local, hidden, color), F32),
        jax.ShapeDtypeStruct((local, code, color), F32),
        jax.ShapeDtypeStruct((local, w_out.shape[1], color), F32),
    ]
    grads = []
    for group in (early, late):
        tables_at, sums_shape, here = (), [], []
        if group is late:
            tables_at = tuple(i for i, (place, _) in enumerate(group) if place // n_sub == 1)
            sums_shape = [jax.ShapeDtypeStruct((rows, cams), F32) for rows in (3, code)]
            here = [relayed]
        grads = pl.pallas_call(
            functools.partial(
                unpack_kernel, tuple(place for place, _ in group), lc, len(grads), packed_rows, tables_at
            ),
            out_shape=shapes + sums_shape,
            in_specs=[vmem] * (len(group) + len(here)) + [hbm] * len(grads),
            out_specs=[hbm] * 4 + [vmem] * len(sums_shape),
            scratch_shapes=[pltpu.VMEM((len(group) * lc,) + a.shape[1:], F32) for a in shapes]
            + [pltpu.SemaphoreType.DMA((len(group) * lc, 4))],
            input_output_aliases={len(group) + len(here) + i: i for i in range(len(grads))},
            compiler_params=params,
            cost_estimate=cost(0),
            name="unpack",
        )(*[value for _, value in group], *here, *grads)
    return tuple(grads)


def solution(mesh):
    samples = ("groups", "cell", "rep", "sub")
    in_specs = (
        P(None, samples),
        P(None, samples),
        P(samples, None),
        P(samples),
        P(samples),
        P("cell", None, None),
        P("cell", None, None),
        P("cell", None, None),
        P("cell", None, None),
        P(None, "cell"),
        P(),
    )
    out_specs = (
        P(("groups", "cell"), None, None),
        P(("groups", "cell"), None, None),
        P(("groups", "cell"), None, None),
        P(("groups", "cell"), None, None),
        P(None, ("groups", "cell")),
        P(None, ("groups", "cell")),
    )
    return jax.shard_map(shards, mesh=mesh, in_specs=in_specs, out_specs=out_specs, check_vma=False)
```

```python
import functools

import jax
import jax.numpy as jnp
from jax import lax
from jax.experimental import pallas as pl
from jax.experimental.pallas import tpu as pltpu
from jax.sharding import PartitionSpec as P

BF16 = jnp.bfloat16
F32 = jnp.float32
VMEM_BYTES = 32 * 1024 * 1024
ALL_VMEM_BYTES = 64 * 1024 * 1024
SLACK_BYTES = 128 * 1024
PART_AXES = ("rep", "sub")
TOGETHER = 2
RECORD = 16
TANGENT_ROW = 8
CAMERA_ROW = 12


def dot_nn(a, b):
    return lax.dot_general(a, b, (((1,), (0,)), ((), ())), preferred_element_type=F32)


def dot_nt(a, b):
    return lax.dot_general(a, b, (((1,), (1,)), ((), ())), preferred_element_type=F32)


def dot_tn(a, b):
    return lax.dot_general(a, b, (((0,), (0,)), ((), ())), preferred_element_type=F32)


def iota(shape, dim):
    return lax.broadcasted_iota(jnp.int32, shape, dim)


def place_kernel(cells_all, cap, n_cell, n_part, *refs):
    sources, placed, arrays, (spread, sems) = refs[:6], refs[6], refs[7:13], refs[13:]
    points_ref, cot_ref, cell_ref, cam_ref, valid_ref, poses_ref = arrays
    lc = cells_all // (n_cell * n_part)
    copies = [
        pltpu.make_async_copy(source, target, sems.at[i])
        for i, (source, target) in enumerate(zip(sources, arrays))
    ]
    for copy in copies:
        copy.start()
    for copy in copies:
        copy.wait()
    n = points_ref.shape[1]
    cams = poses_ref.shape[1]
    cam = cam_ref[...]
    cam_hot = (iota((cams, n), 0) == cam).astype(F32).astype(BF16)
    poses = poses_ref[...]
    high = poses.astype(BF16).astype(F32)
    middle = (poses - high).astype(BF16).astype(F32)
    parts = jnp.concatenate([high, middle, poses - high - middle], axis=0).astype(BF16)
    moved = dot_nn(parts, cam_hot)
    offsets = (moved[0:3] + moved[3:6]) + moved[6:9]
    points = points_ref[...]
    coords = jnp.concatenate([points[0:3] + offsets, points[3:4]], axis=0)
    coords_high = coords.astype(BF16).astype(F32)
    tangent = cot_ref[...] * valid_ref[...].astype(F32)
    record = jnp.concatenate(
        [coords_high, coords - coords_high, tangent, cam.astype(F32), jnp.zeros((3, n), F32)], axis=0
    )
    width = min(256, n)
    blocks = n // width
    upper = (iota((width, width), 0) <= iota((width, width), 1)).astype(F32).astype(BF16)
    cell_of = cell_ref[...]
    hots = [
        (iota((cells_all, width), 0) == cell_of[:, b * width:(b + 1) * width]).astype(F32)
        for b in range(blocks)
    ]
    counts = dot_nn(jnp.concatenate(hots, axis=0).astype(BF16), upper)
    carry = jnp.zeros((cells_all, 1), F32)
    ranks = []
    for b in range(blocks):
        counted = counts[b * cells_all:(b + 1) * cells_all]
        ranks.append(jnp.sum((counted + carry) * hots[b], axis=0, keepdims=True) - 1.0)
        carry = carry + counted[:, width - 1:width]
    rank = jnp.concatenate(ranks, axis=1).astype(jnp.int32)
    rank_hot = (iota((cap, n), 0) == rank).astype(F32).astype(BF16)
    cell_rows = jnp.broadcast_to(cell_of, (RECORD, n))
    for c in range(cells_all):
        owner_cell, owner_part, j = c // (n_part * lc), c // lc % n_part, c % lc
        slot = (owner_part * n_cell + owner_cell) * lc + j
        spread[slot * RECORD:(slot + 1) * RECORD, :] = jnp.where(cell_rows == c, record, 0.0).astype(BF16)
    placed[...] = dot_nt(spread[...], rank_hot).astype(BF16)


def sin_cos(x):
    n = jnp.floor(x * 0.6366197723675814 + 0.5)
    r = ((x - n * 1.5703125) - n * 4.837512969970703125e-4) - n * 7.54978995489188216e-8
    z = r * r
    s = r + (r * z) * (-1.6666654611e-1 + z * (8.3321608736e-3 + z * -1.9515295891e-4))
    c = (1.0 - 0.5 * z) + (z * z) * (
        4.166664568298827e-2 + z * (-1.388731625493765e-3 + z * 2.443315711809948e-5))
    q = n.astype(jnp.int32)
    swap = (q & 1) == 1
    sine = jnp.where(swap, c, s)
    cosine = jnp.where(swap, s, c)
    sine = jnp.where((q & 2) == 2, -sine, sine)
    cosine = jnp.where(((q + 1) & 2) == 2, -cosine, cosine)
    return sine, cosine


def double_angle(s, c):
    return 2.0 * s * c, 1.0 - 2.0 * s * s


def soft(x):
    e = jnp.exp(-jnp.abs(x))
    u = 1.0 + e
    plus = jnp.maximum(x, 0.0) + jnp.where(e < 1e-4, e, jnp.log(u))
    r = pl.reciprocal(u, approx=True)
    return plus, jnp.where(x >= 0.0, r, e * r)


def fold(table, rows):
    return jnp.concatenate([table[r:r + rows] for r in range(0, table.shape[0], rows)], axis=1)


def chunk_steps(freq_count, kc, cols, rec, weights, code_part, w_out_t, kept, results):
    enc_s, gt_s, trunk_s, gc_s, act_s, rec_s = kept
    w_enc, w_enc_t, w_hidden, w_hidden_t = weights
    cams = code_part.shape[1] // 2
    width = rec.shape[1]
    half = freq_count // 2
    scale = jnp.exp2(iota((half, 1), 0).astype(F32) * 0.25)
    top = 2.0 ** (half // 4)
    rec_s[:, cols] = rec
    recf = rec.astype(F32)
    coords = recf[0:4] + recf[4:8]
    cam = recf[CAMERA_ROW:CAMERA_ROW + 1].astype(jnp.int32)
    cam_hot = (iota((cams, width), 0) == cam).astype(F32).astype(BF16)
    angles = jnp.concatenate([coords[i:i + 1] * scale for i in range(4)], axis=0)
    s1, c1 = sin_cos(angles)
    s2, c2 = s1, c1
    for _ in range(half // 4):
        s2, c2 = double_angle(s2, c2)
    pieces = []
    for a, b in ((s1, s2), (c1, c2)):
        for i in range(4):
            pieces += [a[i * half:(i + 1) * half], b[i * half:(i + 1) * half]]
    encoded = jnp.concatenate(pieces, axis=0).astype(BF16)
    enc_s[:, cols] = encoded
    yield
    trunk, slope_trunk = soft(dot_nn(w_enc_t, encoded))
    trunk = trunk.astype(BF16)
    trunk_s[:, cols] = trunk
    yield
    act, slope_color = soft(
        dot_nn(w_hidden_t, trunk) + dot_nn(code_part, jnp.concatenate([cam_hot, cam_hot], axis=0))
    )
    act_s[:, cols] = act.astype(BF16)
    gc = (dot_nn(w_out_t, rec) * slope_color).astype(BF16)
    gc_s[:, cols] = gc
    yield
    gt = (dot_nn(w_hidden, gc) * slope_trunk).astype(BF16)
    gt_s[:, cols] = gt
    camera_color = dot_nt(cam_hot, gc)
    yield
    grad_enc = dot_nn(w_enc, gt)
    sums = []
    for i in range(3):
        a, b = i * 2 * half, (4 + i) * 2 * half
        at = slice(i * half, (i + 1) * half)
        first = grad_enc[a:a + half] * c1[at] - grad_enc[b:b + half] * s1[at]
        second = grad_enc[a + half:a + 2 * half] * c2[at] - grad_enc[b + half:b + 2 * half] * s2[at]
        sums.append(jnp.sum((first + top * second) * scale, axis=0, keepdims=True))
    row = iota((RECORD, width), 0)
    tail = jnp.where(row == 0, sums[0], jnp.where(row == 1, sums[1], jnp.where(row == 2, sums[2], 0.0)))
    results[kc] = (camera_color.astype(BF16), dot_nt(tail.astype(BF16), cam_hot))


def prepare_kernel(n_cell, codes_ref, w_out_ref, *refs):
    sources, own, (w_enc_t_ref, w_hidden_t_ref, w_out_t_ref, coded_ref, sems) = refs[:3], refs[3:6], refs[6:]
    w_enc_ref, w_hidden_ref, w_code_ref = own
    me_part = lax.axis_index(PART_AXES)
    lc = w_enc_ref.shape[0]
    cams = codes_ref.shape[1] // n_cell
    copies = [
        pltpu.make_async_copy(source.at[pl.ds(me_part * lc, lc)], target, sems.at[i])
        for i, (source, target) in enumerate(zip(sources, own))
    ]
    for copy in copies:
        copy.start()
    for copy in copies:
        copy.wait()
    for j in range(lc):
        w_enc_t_ref[j] = w_enc_ref[j].T
        w_hidden_t_ref[j] = w_hidden_ref[j].T
        w_out_t_ref[j] = w_out_ref[me_part * lc + j].T
        coded = dot_tn(w_code_ref[j], codes_ref[...])
        high = coded.astype(BF16)
        low = (coded - high.astype(F32)).astype(BF16)
        for kc in range(n_cell):
            at = slice(kc * cams, (kc + 1) * cams)
            coded_ref[j, kc] = jnp.concatenate([high[:, at], low[:, at]], axis=1)


def cells_kernel(n_cell, freq_count, lc, codes_ref, *refs):
    weights_refs, turned_refs, arrived = refs[:3], refs[3:7], refs[7]
    packed_ref, table_ref, kept_refs, sums = refs[8], refs[9], refs[10:16], refs[16]
    rows = packed_ref.shape[0] // lc
    blocks = arrived.shape[0] // n_cell
    width = blocks * arrived.shape[2]
    codes = codes_ref[...]
    for j in range(lc):
        kept = [k.at[j] for k in kept_refs]
        enc_s, gt_s, trunk_s, gc_s, act_s, rec_s = kept
        w_enc, w_hidden, w_code = (w[j] for w in weights_refs)
        w_enc_t, w_hidden_t, w_out_t, coded = (w.at[j] for w in turned_refs)
        w_out_t = w_out_t[...]
        weights = (w_enc, w_enc_t[...], w_hidden, w_hidden_t[...])
        results = [None] * n_cell
        steps = []
        for kc in range(n_cell):
            rec = jnp.concatenate(
                [arrived[b * n_cell + kc, j * RECORD:(j + 1) * RECORD, :] for b in range(blocks)], axis=1
            )
            cols = slice(kc * width, (kc + 1) * width)
            steps.append(
                chunk_steps(freq_count, kc, cols, rec, weights, coded[kc], w_out_t, kept, results)
            )
        for first in range(0, n_cell, TOGETHER):
            live = steps[first:first + TOGETHER]
            while live:
                live = [step for step in live if next(step, live) is not live]
        for kc in range(n_cell):
            camera_color, camera_pose = results[kc]
            table = jnp.concatenate([dot_nt(w_code, camera_color), camera_pose], axis=0)
            if j:
                table = table + sums[kc]
            if j < lc - 1:
                sums[kc] = table
            else:
                copies = table_ref.shape[0] // n_cell
                for i in range(copies):
                    table_ref[kc * copies + i] = fold(table, table_ref.shape[1]).astype(BF16)
        row = j * rows
        color = gc_s.shape[0]
        g_enc = dot_nt(enc_s[...], gt_s[...]).astype(BF16)
        for part in range(g_enc.shape[1] // color):
            packed_ref[row:row + g_enc.shape[0], :] = g_enc[:, part * color:(part + 1) * color]
            row += g_enc.shape[0]
        hidden, code = trunk_s.shape[0], codes.shape[0]
        packed_ref[row:row + hidden, :] = dot_nt(trunk_s[...], gc_s[...]).astype(BF16)
        row += hidden
        camera_color = jnp.concatenate([result[0] for result in results], axis=0)
        packed_ref[row:row + code, :] = dot_nn(codes, camera_color).astype(BF16)
        row += code
        packed_ref[row:row + RECORD, :] = dot_nt(rec_s[...], act_s[...]).astype(BF16)


def relay_kernel(tables_ref, packed_ref, _, out_ref):
    total = sum(tables_ref[k].astype(F32) for k in range(tables_ref.shape[0]))
    out_ref[0:packed_ref.shape[0], :] = packed_ref[...]
    out_ref[packed_ref.shape[0]:, :] = total.astype(BF16)


def unpack_kernel(places, lc, n_prev, packed_rows, tables_at, *refs):
    ins, refs = refs[:len(places)], refs[len(places):]
    if tables_at:
        here, refs = refs[0], refs[1:]
    outs, refs = refs[n_prev:n_prev + 4], refs[n_prev + 4:]
    camera_outs, refs = (refs[:2], refs[2:]) if tables_at else ((), refs)
    wide, sems = refs[:-1], refs[-1]
    enc_v, hidden_v, code_v, out_v = wide
    enc_rows, enc_cols = enc_v.shape[1:]
    hidden, color = hidden_v.shape[1:]
    code, out_rows = code_v.shape[1], out_v.shape[1]
    me_part = lax.axis_index(PART_AXES)
    copies = []
    for i in range(len(places) * lc):
        cell = (me_part ^ places[i // lc]) * lc + i % lc
        src = ins[i // lc]
        row = i % lc * packed_rows

        def send(m):
            copy = pltpu.make_async_copy(wide[m].at[i], outs[m].at[cell], sems.at[i, m])
            copy.start()
            copies.append(copy)

        for part in range(enc_cols // color):
            enc_v[i, :, part * color:(part + 1) * color] = src[row:row + enc_rows, :].astype(F32)
            row += enc_rows
        send(0)
        hidden_v[i] = src[row:row + hidden, :].astype(F32)
        row += hidden
        send(1)
        code_v[i] = src[row:row + code, :].astype(F32)
        row += code
        out_v[i] = src[row:row + RECORD, :].astype(F32)[TANGENT_ROW:TANGENT_ROW + out_rows]
        send(2)
        send(3)
    if tables_at:
        cams = camera_outs[0].shape[1]
        first = lc * packed_rows
        total = here[first:, :].astype(F32)
        for i in tables_at:
            total = total + ins[i][first:, :].astype(F32)
        total = jnp.concatenate([total[:, c:c + cams] for c in range(0, total.shape[1], cams)], axis=0)
        camera_outs[0][...] = total[code:code + 3]
        camera_outs[1][...] = total[0:code]
    for copy in copies:
        copy.wait()


def cost(us):
    return pl.CostEstimate(flops=us * 10 ** 9, bytes_accessed=us * 3 * 10 ** 6, transcendentals=0)


def exchange(value, axes, count, k):
    if k == 0:
        return value
    return lax.ppermute(value, axes, [(i, i ^ k) for i in range(count)])


def shards(points, cotangent, cell_ids, camera_ids, valid, w_enc, w_hidden, w_code, w_out, poses, codes):
    n_cell, n_rep, n_sub = lax.axis_size("cell"), lax.axis_size("rep"), lax.axis_size("sub")
    n_part = n_rep * n_sub
    local = w_enc.shape[0]
    lc = local // n_part
    cells_all = local * n_cell
    n = points.shape[1]
    cap = max(2, 2 * n // cells_all)
    enc, hidden = w_enc.shape[1:]
    color = w_hidden.shape[2]
    freq_count = enc // 8
    cams = poses.shape[1]
    code = codes.shape[0]
    width = n_part * cap
    params = pltpu.CompilerParams(vmem_limit_bytes=VMEM_BYTES)
    vmem = pl.BlockSpec(memory_space=pltpu.VMEM)
    hbm = pl.BlockSpec(memory_space=pltpu.HBM)

    inputs = (points, cotangent, cell_ids.reshape(1, n), camera_ids.reshape(1, n), valid.reshape(1, n), poses)
    weights = (w_enc, w_hidden, w_code)
    slots_all = cells_all * RECORD
    room = 2 * slots_all * max(cap, 128) + SLACK_BYTES
    sent = pl.pallas_call(
        functools.partial(place_kernel, cells_all, cap, n_cell, n_part),
        out_shape=jax.ShapeDtypeStruct((slots_all, cap), BF16),
        in_specs=[hbm] * 6,
        out_specs=vmem,
        scratch_shapes=[pltpu.VMEM(a.shape, a.dtype) for a in inputs]
        + [pltpu.VMEM((slots_all, n), BF16), pltpu.SemaphoreType.DMA((6,))],
        compiler_params=pltpu.CompilerParams(vmem_limit_bytes=ALL_VMEM_BYTES - room),
        cost_estimate=cost(3),
        name="place",
    )(*inputs)

    w_out_rows = jnp.pad(w_out, ((0, 0), (TANGENT_ROW, RECORD - TANGENT_ROW - w_out.shape[1]), (0, 0)))

    arrived = lax.all_to_all(
        sent.reshape(n_cell * n_part, lc * RECORD, cap), PART_AXES + ("cell",), 0, 0, tiled=True
    )
    if cap % 128:
        arrived = arrived.reshape(n_part, n_cell, lc * RECORD, cap).transpose(1, 2, 0, 3)
        arrived = arrived.reshape(n_cell, lc * RECORD, width)

    packed_rows = enc * (hidden // color) + hidden + code + RECORD
    slots = n_cell * width
    kept_rows = (enc, hidden, hidden, color, color, RECORD)
    table_shape = (n_cell, code + RECORD, cams)
    folded = (table_shape[1] * cams // color, color)
    own_weights = pl.pallas_call(
        functools.partial(prepare_kernel, n_cell),
        in_specs=[vmem] * 2 + [hbm] * 3,
        out_specs=[vmem] * 7,
        out_shape=[jax.ShapeDtypeStruct((lc,) + w.shape[1:], BF16) for w in weights] + [
            jax.ShapeDtypeStruct((lc, hidden, enc), BF16),
            jax.ShapeDtypeStruct((lc, color, hidden), BF16),
            jax.ShapeDtypeStruct((lc, color, RECORD), BF16),
            jax.ShapeDtypeStruct((lc, n_cell, color, 2 * cams), BF16),
        ],
        scratch_shapes=[pltpu.SemaphoreType.DMA((3,))],
        compiler_params=params,
        cost_estimate=cost(2),
        name="prepare",
    )(codes, w_out_rows, *weights)
    packed, table = pl.pallas_call(
        functools.partial(cells_kernel, n_cell, freq_count, lc),
        in_specs=[vmem] * 9,
        out_specs=[vmem, vmem],
        out_shape=[
            jax.ShapeDtypeStruct((lc * packed_rows, color), BF16),
            jax.ShapeDtypeStruct((n_cell * n_rep,) + folded, BF16),
        ],
        scratch_shapes=[pltpu.VMEM((lc, r, slots), BF16) for r in kept_rows] + [pltpu.VMEM(table_shape, F32)],
        compiler_params=params,
        cost_estimate=cost(10),
        name="cells",
    )(codes, *own_weights, arrived)

    over_rep = [exchange(packed, "rep", n_rep, kr) for kr in range(n_rep)]
    over_sub = [exchange(packed, "sub", n_sub, ks) for ks in range(n_sub)]
    tables = lax.all_to_all(table, ("cell", "rep"), 0, 0, tiled=True)
    relayed = pl.pallas_call(
        relay_kernel,
        in_specs=[vmem] * 3,
        out_specs=vmem,
        out_shape=jax.ShapeDtypeStruct((lc * packed_rows + folded[0], color), BF16),
        compiler_params=params,
        cost_estimate=cost(0),
        name="relay",
    )(tables, over_rep[1], over_sub[-1])

    early, late = [], []
    for kr in range(n_rep):
        for ks in range(n_sub):
            if kr == 0:
                early.append((ks, over_sub[ks]))
            elif ks == 0:
                early.append((kr * n_sub, over_rep[kr]))
            else:
                sent_on = relayed if kr == 1 else over_rep[kr]
                late.append((kr * n_sub + ks, exchange(sent_on, "sub", n_sub, ks)))
    shapes = [
        jax.ShapeDtypeStruct((local, enc, hidden), F32),
        jax.ShapeDtypeStruct((local, hidden, color), F32),
        jax.ShapeDtypeStruct((local, code, color), F32),
        jax.ShapeDtypeStruct((local, w_out.shape[1], color), F32),
    ]
    grads = []
    for group in (early, late):
        tables_at, sums_shape, here = (), [], []
        if group is late:
            tables_at = tuple(i for i, (place, _) in enumerate(group) if place // n_sub == 1)
            sums_shape = [jax.ShapeDtypeStruct((rows, cams), F32) for rows in (3, code)]
            here = [relayed]
        grads = pl.pallas_call(
            functools.partial(
                unpack_kernel, tuple(place for place, _ in group), lc, len(grads), packed_rows, tables_at
            ),
            out_shape=shapes + sums_shape,
            in_specs=[vmem] * (len(group) + len(here)) + [hbm] * len(grads),
            out_specs=[hbm] * 4 + [vmem] * len(sums_shape),
            scratch_shapes=[pltpu.VMEM((len(group) * lc,) + a.shape[1:], F32) for a in shapes]
            + [pltpu.SemaphoreType.DMA((len(group) * lc, 4))],
            input_output_aliases={len(group) + len(here) + i: i for i in range(len(grads))},
            compiler_params=params,
            cost_estimate=cost(0),
            name="unpack",
        )(*[value for _, value in group], *here, *grads)
    return tuple(grads)


def solution(mesh):
    samples = ("groups", "cell", "rep", "sub")
    in_specs = (
        P(None, samples),
        P(None, samples),
        P(samples, None),
        P(samples),
        P(samples),
        P("cell", None, None),
        P("cell", None, None),
        P("cell", None, None),
        P("cell", None, None),
        P(None, "cell"),
        P(),
    )
    out_specs = (
        P(("groups", "cell"), None, None),
        P(("groups", "cell"), None, None),
        P(("groups", "cell"), None, None),
        P(("groups", "cell"), None, None),
        P(None, ("groups", "cell")),
        P(None, ("groups", "cell")),
    )
    return jax.shard_map(shards, mesh=mesh, in_specs=in_specs, out_specs=out_specs, check_vma=False)
```

```python
import functools

import jax
import jax.numpy as jnp
from jax import lax
from jax.experimental import pallas as pl
from jax.experimental.pallas import tpu as pltpu
from jax.sharding import PartitionSpec as P

BF16 = jnp.bfloat16
F32 = jnp.float32
VMEM_BYTES = 32 * 1024 * 1024
ALL_VMEM_BYTES = 64 * 1024 * 1024
SLACK_BYTES = 128 * 1024
PART_AXES = ("rep", "sub")
TOGETHER = 2
RECORD = 16
TANGENT_ROW = 8
CAMERA_ROW = 12


def dot_nn(a, b):
    return lax.dot_general(a, b, (((1,), (0,)), ((), ())), preferred_element_type=F32)


def dot_nt(a, b):
    return lax.dot_general(a, b, (((1,), (1,)), ((), ())), preferred_element_type=F32)


def dot_tn(a, b):
    return lax.dot_general(a, b, (((0,), (0,)), ((), ())), preferred_element_type=F32)


def iota(shape, dim):
    return lax.broadcasted_iota(jnp.int32, shape, dim)


def place_kernel(cells_all, cap, n_cell, n_part, *refs):
    sources, placed, arrays, (spread, sems) = refs[:6], refs[6], refs[7:13], refs[13:]
    points_ref, cot_ref, cell_ref, cam_ref, valid_ref, poses_ref = arrays
    lc = cells_all // (n_cell * n_part)
    copies = [
        pltpu.make_async_copy(source, target, sems.at[i])
        for i, (source, target) in enumerate(zip(sources, arrays))
    ]
    for copy in copies:
        copy.start()
    for copy in copies:
        copy.wait()
    n = points_ref.shape[1]
    cams = poses_ref.shape[1]
    cam = cam_ref[...]
    cam_hot = (iota((cams, n), 0) == cam).astype(F32).astype(BF16)
    poses = poses_ref[...]
    high = poses.astype(BF16).astype(F32)
    middle = (poses - high).astype(BF16).astype(F32)
    parts = jnp.concatenate([high, middle, poses - high - middle], axis=0).astype(BF16)
    moved = dot_nn(parts, cam_hot)
    offsets = (moved[0:3] + moved[3:6]) + moved[6:9]
    points = points_ref[...]
    coords = jnp.concatenate([points[0:3] + offsets, points[3:4]], axis=0)
    coords_high = coords.astype(BF16).astype(F32)
    tangent = cot_ref[...] * valid_ref[...].astype(F32)
    record = jnp.concatenate(
        [coords_high, coords - coords_high, tangent, cam.astype(F32), jnp.zeros((3, n), F32)], axis=0
    )
    width = min(256, n)
    blocks = n // width
    upper = (iota((width, width), 0) <= iota((width, width), 1)).astype(F32).astype(BF16)
    cell_of = cell_ref[...]
    hots = [
        (iota((cells_all, width), 0) == cell_of[:, b * width:(b + 1) * width]).astype(F32)
        for b in range(blocks)
    ]
    counts = dot_nn(jnp.concatenate(hots, axis=0).astype(BF16), upper)
    carry = jnp.zeros((cells_all, 1), F32)
    ranks = []
    for b in range(blocks):
        counted = counts[b * cells_all:(b + 1) * cells_all]
        ranks.append(jnp.sum((counted + carry) * hots[b], axis=0, keepdims=True) - 1.0)
        carry = carry + counted[:, width - 1:width]
    rank = jnp.concatenate(ranks, axis=1).astype(jnp.int32)
    rank_hot = (iota((cap, n), 0) == rank).astype(F32).astype(BF16)
    cell_rows = jnp.broadcast_to(cell_of, (RECORD, n))
    for c in range(cells_all):
        owner_cell, owner_part, j = c // (n_part * lc), c // lc % n_part, c % lc
        slot = (owner_part * n_cell + owner_cell) * lc + j
        spread[slot * RECORD:(slot + 1) * RECORD, :] = jnp.where(cell_rows == c, record, 0.0).astype(BF16)
    placed[...] = dot_nt(spread[...], rank_hot).astype(BF16)


def sin_cos(x):
    n = jnp.floor(x * 0.6366197723675814 + 0.5)
    r = ((x - n * 1.5703125) - n * 4.837512969970703125e-4) - n * 7.54978995489188216e-8
    z = r * r
    s = r + (r * z) * (-1.6666654611e-1 + z * (8.3321608736e-3 + z * -1.9515295891e-4))
    c = (1.0 - 0.5 * z) + (z * z) * (
        4.166664568298827e-2 + z * (-1.388731625493765e-3 + z * 2.443315711809948e-5))
    q = n.astype(jnp.int32)
    swap = (q & 1) == 1
    sine = jnp.where(swap, c, s)
    cosine = jnp.where(swap, s, c)
    sine = jnp.where((q & 2) == 2, -sine, sine)
    cosine = jnp.where(((q + 1) & 2) == 2, -cosine, cosine)
    return sine, cosine


def double_angle(s, c):
    return 2.0 * s * c, 1.0 - 2.0 * s * s


def soft(x):
    e = jnp.exp(-jnp.abs(x))
    u = 1.0 + e
    plus = jnp.maximum(x, 0.0) + jnp.where(e < 1e-4, e, jnp.log(u))
    r = pl.reciprocal(u, approx=True)
    return plus, jnp.where(x >= 0.0, r, e * r)


def fold(table, rows):
    return jnp.concatenate([table[r:r + rows] for r in range(0, table.shape[0], rows)], axis=1)


def chunk_steps(freq_count, kc, cols, rec, weights, code_part, w_out_t, kept, results):
    enc_s, gt_s, trunk_s, gc_s, act_s, rec_s = kept
    w_enc, w_enc_t, w_hidden, w_hidden_t = weights
    cams = code_part.shape[1] // 2
    width = rec.shape[1]
    half = freq_count // 2
    scale = jnp.exp2(iota((half, 1), 0).astype(F32) * 0.25)
    top = 2.0 ** (half // 4)
    rec_s[:, cols] = rec
    recf = rec.astype(F32)
    coords = recf[0:4] + recf[4:8]
    cam = recf[CAMERA_ROW:CAMERA_ROW + 1].astype(jnp.int32)
    cam_hot = (iota((cams, width), 0) == cam).astype(F32).astype(BF16)
    angles = jnp.concatenate([coords[i:i + 1] * scale for i in range(4)], axis=0)
    s1, c1 = sin_cos(angles)
    s2, c2 = s1, c1
    for _ in range(half // 4):
        s2, c2 = double_angle(s2, c2)
    pieces = []
    for a, b in ((s1, s2), (c1, c2)):
        for i in range(4):
            pieces += [a[i * half:(i + 1) * half], b[i * half:(i + 1) * half]]
    encoded = jnp.concatenate(pieces, axis=0).astype(BF16)
    enc_s[:, cols] = encoded
    yield
    trunk, slope_trunk = soft(dot_nn(w_enc_t, encoded))
    trunk = trunk.astype(BF16)
    trunk_s[:, cols] = trunk
    yield
    act, slope_color = soft(
        dot_nn(w_hidden_t, trunk) + dot_nn(code_part, jnp.concatenate([cam_hot, cam_hot], axis=0))
    )
    act_s[:, cols] = act.astype(BF16)
    gc = (dot_nn(w_out_t, rec) * slope_color).astype(BF16)
    gc_s[:, cols] = gc
    yield
    gt = (dot_nn(w_hidden, gc) * slope_trunk).astype(BF16)
    gt_s[:, cols] = gt
    camera_color = dot_nt(cam_hot, gc)
    yield
    grad_enc = dot_nn(w_enc, gt)
    sums = []
    for i in range(3):
        a, b = i * 2 * half, (4 + i) * 2 * half
        at = slice(i * half, (i + 1) * half)
        first = grad_enc[a:a + half] * c1[at] - grad_enc[b:b + half] * s1[at]
        second = grad_enc[a + half:a + 2 * half] * c2[at] - grad_enc[b + half:b + 2 * half] * s2[at]
        sums.append(jnp.sum((first + top * second) * scale, axis=0, keepdims=True))
    row = iota((RECORD, width), 0)
    tail = jnp.where(row == 0, sums[0], jnp.where(row == 1, sums[1], jnp.where(row == 2, sums[2], 0.0)))
    results[kc] = (camera_color.astype(BF16), dot_nt(tail.astype(BF16), cam_hot))


def prepare_kernel(n_cell, codes_ref, w_out_ref, *refs):
    sources, own, (w_enc_t_ref, w_hidden_t_ref, w_out_t_ref, coded_ref, sems) = refs[:3], refs[3:6], refs[6:]
    w_enc_ref, w_hidden_ref, w_code_ref = own
    me_part = lax.axis_index(PART_AXES)
    lc = w_enc_ref.shape[0]
    cams = codes_ref.shape[1] // n_cell
    copies = [
        pltpu.make_async_copy(source.at[pl.ds(me_part * lc, lc)], target, sems.at[i])
        for i, (source, target) in enumerate(zip(sources, own))
    ]
    for copy in copies:
        copy.start()
    for copy in copies:
        copy.wait()
    for j in range(lc):
        w_enc_t_ref[j] = w_enc_ref[j].T
        w_hidden_t_ref[j] = w_hidden_ref[j].T
        w_out_t_ref[j] = w_out_ref[me_part * lc + j].T
        coded = dot_tn(w_code_ref[j], codes_ref[...])
        high = coded.astype(BF16)
        low = (coded - high.astype(F32)).astype(BF16)
        for kc in range(n_cell):
            at = slice(kc * cams, (kc + 1) * cams)
            coded_ref[j, kc] = jnp.concatenate([high[:, at], low[:, at]], axis=1)


def cells_kernel(n_cell, freq_count, lc, codes_ref, *refs):
    weights_refs, turned_refs, arrived = refs[:3], refs[3:7], refs[7]
    packed_ref, table_ref, kept_refs, sums = refs[8], refs[9], refs[10:16], refs[16]
    rows = packed_ref.shape[0] // lc
    blocks = arrived.shape[0] // n_cell
    width = blocks * arrived.shape[2]
    codes = codes_ref[...]
    for j in range(lc):
        kept = [k.at[j] for k in kept_refs]
        enc_s, gt_s, trunk_s, gc_s, act_s, rec_s = kept
        w_enc, w_hidden, w_code = (w[j] for w in weights_refs)
        w_enc_t, w_hidden_t, w_out_t, coded = (w.at[j] for w in turned_refs)
        w_out_t = w_out_t[...]
        weights = (w_enc, w_enc_t[...], w_hidden, w_hidden_t[...])
        results = [None] * n_cell
        steps = []
        for kc in range(n_cell):
            rec = jnp.concatenate(
                [arrived[b * n_cell + kc, j * RECORD:(j + 1) * RECORD, :] for b in range(blocks)], axis=1
            )
            cols = slice(kc * width, (kc + 1) * width)
            steps.append(
                chunk_steps(freq_count, kc, cols, rec, weights, coded[kc], w_out_t, kept, results)
            )
        for first in range(0, n_cell, TOGETHER):
            live = steps[first:first + TOGETHER]
            while live:
                live = [step for step in live if next(step, live) is not live]
        for kc in range(n_cell):
            camera_color, camera_pose = results[kc]
            table = jnp.concatenate([dot_nt(w_code, camera_color), camera_pose], axis=0)
            if j:
                table = table + sums[kc]
            if j < lc - 1:
                sums[kc] = table
            else:
                copies = table_ref.shape[0] // n_cell
                for i in range(copies):
                    table_ref[kc * copies + i] = fold(table, table_ref.shape[1]).astype(BF16)
        row = j * rows
        color = gc_s.shape[0]
        g_enc = dot_nt(enc_s[...], gt_s[...]).astype(BF16)
        for part in range(g_enc.shape[1] // color):
            packed_ref[row:row + g_enc.shape[0], :] = g_enc[:, part * color:(part + 1) * color]
            row += g_enc.shape[0]
        hidden, code = trunk_s.shape[0], codes.shape[0]
        packed_ref[row:row + hidden, :] = dot_nt(trunk_s[...], gc_s[...]).astype(BF16)
        row += hidden
        camera_color = jnp.concatenate([result[0] for result in results], axis=0)
        packed_ref[row:row + code, :] = dot_nn(codes, camera_color).astype(BF16)
        row += code
        packed_ref[row:row + RECORD, :] = dot_nt(rec_s[...], act_s[...]).astype(BF16)


def relay_kernel(tables_ref, packed_ref, _, out_ref):
    total = sum(tables_ref[k].astype(F32) for k in range(tables_ref.shape[0]))
    out_ref[0:packed_ref.shape[0], :] = packed_ref[...]
    out_ref[packed_ref.shape[0]:, :] = total.astype(BF16)


def unpack_kernel(places, lc, n_prev, packed_rows, tables_at, *refs):
    ins, refs = refs[:len(places)], refs[len(places):]
    if tables_at:
        here, refs = refs[0], refs[1:]
    outs, refs = refs[n_prev:n_prev + 4], refs[n_prev + 4:]
    camera_outs, refs = (refs[:2], refs[2:]) if tables_at else ((), refs)
    wide, sems, refs = refs[:4], refs[4], refs[5:]
    enc_v, hidden_v, code_v, out_v = wide
    enc_rows, enc_cols = enc_v.shape[1:]
    hidden, color = hidden_v.shape[1:]
    code, out_rows = code_v.shape[1], out_v.shape[1]
    me_part = lax.axis_index(PART_AXES)
    copies = []
    if tables_at:
        cams = camera_outs[0].shape[1]
        first = lc * packed_rows
        total = here[first:, :].astype(F32)
        for i in tables_at:
            total = total + ins[i][first:, :].astype(F32)
        total = jnp.concatenate([total[:, c:c + cams] for c in range(0, total.shape[1], cams)], axis=0)
        camera_sems = refs[2]
        refs[0][...] = total[code:code + 3]
        refs[1][...] = total[0:code]
        for m in range(2):
            copy = pltpu.make_async_copy(refs[m], camera_outs[m], camera_sems.at[m])
            copy.start()
            copies.append(copy)
    for i in range(len(places) * lc):
        cell = (me_part ^ places[i // lc]) * lc + i % lc
        src = ins[i // lc]
        row = i % lc * packed_rows

        def send(m):
            copy = pltpu.make_async_copy(wide[m].at[i], outs[m].at[cell], sems.at[i, m])
            copy.start()
            copies.append(copy)

        for part in range(enc_cols // color):
            enc_v[i, :, part * color:(part + 1) * color] = src[row:row + enc_rows, :].astype(F32)
            row += enc_rows
        send(0)
        hidden_v[i] = src[row:row + hidden, :].astype(F32)
        row += hidden
        send(1)
        code_v[i] = src[row:row + code, :].astype(F32)
        row += code
        out_v[i] = src[row:row + RECORD, :].astype(F32)[TANGENT_ROW:TANGENT_ROW + out_rows]
        send(2)
        send(3)
    for copy in copies:
        copy.wait()


def cost(us):
    return pl.CostEstimate(flops=us * 10 ** 9, bytes_accessed=us * 3 * 10 ** 6, transcendentals=0)


def exchange(value, axes, count, k):
    if k == 0:
        return value
    return lax.ppermute(value, axes, [(i, i ^ k) for i in range(count)])


def shards(points, cotangent, cell_ids, camera_ids, valid, w_enc, w_hidden, w_code, w_out, poses, codes):
    n_cell, n_rep, n_sub = lax.axis_size("cell"), lax.axis_size("rep"), lax.axis_size("sub")
    n_part = n_rep * n_sub
    local = w_enc.shape[0]
    lc = local // n_part
    cells_all = local * n_cell
    n = points.shape[1]
    cap = max(2, 2 * n // cells_all)
    enc, hidden = w_enc.shape[1:]
    color = w_hidden.shape[2]
    freq_count = enc // 8
    cams = poses.shape[1]
    code = codes.shape[0]
    width = n_part * cap
    params = pltpu.CompilerParams(vmem_limit_bytes=VMEM_BYTES)
    vmem = pl.BlockSpec(memory_space=pltpu.VMEM)
    hbm = pl.BlockSpec(memory_space=pltpu.HBM)

    inputs = (points, cotangent, cell_ids.reshape(1, n), camera_ids.reshape(1, n), valid.reshape(1, n), poses)
    weights = (w_enc, w_hidden, w_code)
    slots_all = cells_all * RECORD
    room = 2 * slots_all * max(cap, 128) + SLACK_BYTES
    sent = pl.pallas_call(
        functools.partial(place_kernel, cells_all, cap, n_cell, n_part),
        out_shape=jax.ShapeDtypeStruct((slots_all, cap), BF16),
        in_specs=[hbm] * 6,
        out_specs=vmem,
        scratch_shapes=[pltpu.VMEM(a.shape, a.dtype) for a in inputs]
        + [pltpu.VMEM((slots_all, n), BF16), pltpu.SemaphoreType.DMA((6,))],
        compiler_params=pltpu.CompilerParams(vmem_limit_bytes=ALL_VMEM_BYTES - room),
        cost_estimate=cost(3),
        name="place",
    )(*inputs)

    w_out_rows = jnp.pad(w_out, ((0, 0), (TANGENT_ROW, RECORD - TANGENT_ROW - w_out.shape[1]), (0, 0)))

    arrived = lax.all_to_all(
        sent.reshape(n_cell * n_part, lc * RECORD, cap), PART_AXES + ("cell",), 0, 0, tiled=True
    )
    if cap % 128:
        arrived = arrived.reshape(n_part, n_cell, lc * RECORD, cap).transpose(1, 2, 0, 3)
        arrived = arrived.reshape(n_cell, lc * RECORD, width)

    packed_rows = enc * (hidden // color) + hidden + code + RECORD
    slots = n_cell * width
    kept_rows = (enc, hidden, hidden, color, color, RECORD)
    table_shape = (n_cell, code + RECORD, cams)
    folded = (table_shape[1] * cams // color, color)
    own_weights = pl.pallas_call(
        functools.partial(prepare_kernel, n_cell),
        in_specs=[vmem] * 2 + [hbm] * 3,
        out_specs=[vmem] * 7,
        out_shape=[jax.ShapeDtypeStruct((lc,) + w.shape[1:], BF16) for w in weights] + [
            jax.ShapeDtypeStruct((lc, hidden, enc), BF16),
            jax.ShapeDtypeStruct((lc, color, hidden), BF16),
            jax.ShapeDtypeStruct((lc, color, RECORD), BF16),
            jax.ShapeDtypeStruct((lc, n_cell, color, 2 * cams), BF16),
        ],
        scratch_shapes=[pltpu.SemaphoreType.DMA((3,))],
        compiler_params=params,
        cost_estimate=cost(2),
        name="prepare",
    )(codes, w_out_rows, *weights)
    packed, table = pl.pallas_call(
        functools.partial(cells_kernel, n_cell, freq_count, lc),
        in_specs=[vmem] * 9,
        out_specs=[vmem, vmem],
        out_shape=[
            jax.ShapeDtypeStruct((lc * packed_rows, color), BF16),
            jax.ShapeDtypeStruct((n_cell * n_rep,) + folded, BF16),
        ],
        scratch_shapes=[pltpu.VMEM((lc, r, slots), BF16) for r in kept_rows] + [pltpu.VMEM(table_shape, F32)],
        compiler_params=params,
        cost_estimate=cost(10),
        name="cells",
    )(codes, *own_weights, arrived)

    over_rep = [exchange(packed, "rep", n_rep, kr) for kr in range(n_rep)]
    over_sub = [exchange(packed, "sub", n_sub, ks) for ks in range(n_sub)]
    tables = lax.all_to_all(table, ("cell", "rep"), 0, 0, tiled=True)
    relayed = pl.pallas_call(
        relay_kernel,
        in_specs=[vmem] * 3,
        out_specs=vmem,
        out_shape=jax.ShapeDtypeStruct((lc * packed_rows + folded[0], color), BF16),
        compiler_params=params,
        cost_estimate=cost(0),
        name="relay",
    )(tables, over_rep[1], over_sub[-1])

    early, late = [], []
    for kr in range(n_rep):
        for ks in range(n_sub):
            if kr == 0:
                early.append((ks, over_sub[ks]))
            elif ks == 0:
                early.append((kr * n_sub, over_rep[kr]))
            else:
                sent_on = relayed if kr == 1 else over_rep[kr]
                late.append((kr * n_sub + ks, exchange(sent_on, "sub", n_sub, ks)))
    shapes = [
        jax.ShapeDtypeStruct((local, enc, hidden), F32),
        jax.ShapeDtypeStruct((local, hidden, color), F32),
        jax.ShapeDtypeStruct((local, code, color), F32),
        jax.ShapeDtypeStruct((local, w_out.shape[1], color), F32),
    ]
    grads = []
    for group in (early, late):
        tables_at, sums_shape, here = (), [], []
        if group is late:
            tables_at = tuple(i for i, (place, _) in enumerate(group) if place // n_sub == 1)
            sums_shape = [jax.ShapeDtypeStruct((rows, cams), F32) for rows in (3, code)]
            here = [relayed]
        grads = pl.pallas_call(
            functools.partial(
                unpack_kernel, tuple(place for place, _ in group), lc, len(grads), packed_rows, tables_at
            ),
            out_shape=shapes + sums_shape,
            in_specs=[vmem] * (len(group) + len(here)) + [hbm] * len(grads),
            out_specs=[hbm] * (4 + len(sums_shape)),
            scratch_shapes=[pltpu.VMEM((len(group) * lc,) + a.shape[1:], F32) for a in shapes]
            + [pltpu.SemaphoreType.DMA((len(group) * lc, 4))]
            + [pltpu.VMEM(a.shape, a.dtype) for a in sums_shape]
            + ([pltpu.SemaphoreType.DMA((2,))] if sums_shape else []),
            input_output_aliases={len(group) + len(here) + i: i for i in range(len(grads))},
            compiler_params=params,
            cost_estimate=cost(0),
            name="unpack",
        )(*[value for _, value in group], *here, *grads)
    return tuple(grads)


def solution(mesh):
    samples = ("groups", "cell", "rep", "sub")
    in_specs = (
        P(None, samples),
        P(None, samples),
        P(samples, None),
        P(samples),
        P(samples),
        P("cell", None, None),
        P("cell", None, None),
        P("cell", None, None),
        P("cell", None, None),
        P(None, "cell"),
        P(),
    )
    out_specs = (
        P(("groups", "cell"), None, None),
        P(("groups", "cell"), None, None),
        P(("groups", "cell"), None, None),
        P(("groups", "cell"), None, None),
        P(None, ("groups", "cell")),
        P(None, ("groups", "cell")),
    )
    return jax.shard_map(shards, mesh=mesh, in_specs=in_specs, out_specs=out_specs, check_vma=False)
```
